256 devices in a mesh: fsdp: 8 (over z), section: 4 (over x), tp: 8 (over y, core).
Axes of the slice: x: 4, y: 4, z: 8, core: 2. Of those that a mesh axis runs over, the one named last changes fastest.
Arguments:
- train_weights: bfloat16 [12, 5120, 10240], P(None, ('fsdp', 'section'), 'tp'), may hold values from -1 to 1
- section_layers: int32 [4], replicated, may hold values from 1 to 5, 12 in all
- prompt_embeds: bfloat16 [16, 64, 5120], P('fsdp'), may hold values from -2.5 to 2.5
- prompt_lengths: int32 [16], P('fsdp'), may hold values from 1 to 64, 768 in all
Outputs:
- section_out: bfloat16 [4, 16, 64, 5120], P('section', 'fsdp', 'tp')
- kv_cache: bfloat16 [4, 16, 64, 2, 1024], P('section', 'fsdp', None, None, 'tp')
The draws below stay inside these ranges and needn't reach their ends.
Inputs may be any that keep to these rules, and one draw needn't show every extreme that they name: `section_layers`: every section has one or more layers and they sum to 12; some section has exactly 5. `prompt_lengths`: some prompt has all 64 positions live.
All inputs are finite; a program needn't handle non-finite values. No bound on the sum of `prompt_lengths` on one device may be relied on, other than what follows from the above.
Results may differ from the reference program's by a relative error of at most 0.027.
Values may be sent and summed in bfloat16 or wider, within the bound.
No kernel may reach another device: no remote copies, remote signals or barrier semaphores. Data moves between devices by JAX's collectives and lax.ppermute only.
A program may use at most 128 MiB of HBM per device.

```python
import math
import jax
import jax.numpy as jnp
import numpy as np
from jax import lax

D = 5120
QH = 32
KVH = 8
HD = 128
LAYERS = 12
MOST_LAYERS = 5
SEQ = 64
BATCH = 16
QDD = 512
UNIT = 1280
COLS = 10240
N_SECTION = 4
N_TP = 8


def draw_train_weights(key, part):
    key = jax.random.fold_in(key, 11)
    column = jnp.arange(COLS) % UNIT
    is_query = column < QDD
    base_vals = jnp.clip(jax.random.normal(key, (LAYERS, D, COLS), jnp.float32), -4.0, 4.0)
    column_scale = jnp.where(is_query, 1.0, 0.5)
    return (base_vals * column_scale * (1.0 / math.sqrt(D))).astype(jnp.bfloat16)


def levels(key, extent, shards, least, largest):
    gain = 1.0
    for axis_at, parts in shards:
        heights = jax.random.uniform(jax.random.fold_in(jax.random.fold_in(key, 6), axis_at), (parts,), jnp.float32, least / len(shards), largest / len(shards))
        gain = gain * jnp.repeat(jnp.exp(heights), extent[axis_at] // parts).reshape((-1,) + (1,) * (len(extent) - 1 - axis_at))
    return gain


def length_profile(amount, total, most, lean):
    weights = [(1 << 20) // math.isqrt(rank ** lean) + 1 for rank in range(2, amount + 1)]
    rest, given = total - most - (amount - 1), [1] * (amount - 1)
    while rest > 0:
        free = [i for i in range(amount - 1) if given[i] < most]
        pool, budget = sum([weights[i] for i in free]), rest
        for i in free:
            extra = min(most - given[i], max(1, budget * weights[i] // pool), rest)
            given[i] = given[i] + extra
            rest = rest - extra
    return np.array([most] + given)


def uneven_parts(key, count, total, bound, lean):
    if count == 2:
        one = jax.random.randint(key, (), max(1, total - bound), min(bound, total - 1) + 1)
        return jnp.stack([one, total - one])
    lengths = jnp.asarray(length_profile(count, total, bound, lean), jnp.int32)
    twos = (count - 1) // 2
    source_of, receiver = lengths[1:1 + 2 * twos:2], lengths[2:2 + 2 * twos:2]
    slack = jnp.minimum(source_of - 1, bound - receiver)
    moved = jax.random.randint(jax.random.fold_in(key, 1), (twos,), 0, 1 << 20) % (slack + 1)
    lengths = lengths.at[1:1 + 2 * twos:2].set(source_of - moved).at[2:2 + 2 * twos:2].set(receiver + moved)
    return lengths[jax.random.permutation(jax.random.fold_in(key, 2), count)]


def noise(rng, shape, spread, most, pieces=(), kind=jnp.bfloat16):
    array = spread * jax.random.normal(rng, shape, jnp.float32)
    if pieces:
        array = array * levels(rng, shape, pieces, -0.22, 0.18)
    return jnp.clip(array, -most, most).astype(kind)


def setup_inputs(seed: int = 0) -> dict:
    seeds = jax.random.split(jax.random.key(seed), 5)
    return {
        "train_weights": draw_train_weights(jax.random.fold_in(seeds[4], 71), 0),
        "section_layers": uneven_parts(seeds[1], N_SECTION, LAYERS, MOST_LAYERS, 0).astype(jnp.int32),
        "prompt_embeds": noise(seeds[2], (BATCH, SEQ, D), 0.3, 2.5, ((0, 8),)),
        "prompt_lengths": uneven_parts(seeds[3], BATCH, BATCH * SEQ * 3 // 4, SEQ, 0).astype(jnp.int32),
    }


rope_base = 1000000.0

def rms_rows(values):
    widened = values.astype(jnp.float32)
    factor = lax.rsqrt(lax.optimization_barrier(jnp.mean(widened * widened, axis=-1, keepdims=True)) + 1e-06)
    return (widened * factor).astype(jnp.bfloat16)

def rotate(head_vals):
    n_rows = head_vals.shape[0]
    half_dim = head_vals.shape[2] // 2
    frequency = rope_base ** (-2.0 * jnp.arange(half_dim, dtype=jnp.float32) / head_vals.shape[2])
    angles = jnp.arange(n_rows, dtype=jnp.float32)[:, None] * frequency[None, :]
    cosine = jnp.cos(angles)[:, None, :]
    sine_part = jnp.sin(angles)[:, None, :]
    front_half = head_vals[..., :half_dim]
    back_half = head_vals[..., half_dim:]
    return jnp.concatenate([front_half * cosine - back_half * sine_part, back_half * cosine + front_half * sine_part], axis=-1)

def attend(queries, key_heads, value_heads, length):
    seq_len = queries.shape[0]
    kv_heads = key_heads.shape[1]
    group_size = queries.shape[1] // kv_heads
    grouped = queries.reshape(seq_len, kv_heads, group_size, queries.shape[2]).astype(jnp.float32)
    scores = jnp.einsum('qhgd,khd->hgqk', grouped, key_heads.astype(jnp.float32)) * queries.shape[2] ** (-0.5)
    row_index = jnp.arange(seq_len)[:, None]
    col_index = jnp.arange(seq_len)[None, :]
    allowed = (col_index <= row_index) & (col_index < length)
    scores = jnp.where(allowed, scores, -1e+30)
    row_top = lax.optimization_barrier(jnp.max(scores, axis=-1, keepdims=True))
    weights_raw = jnp.where(allowed, jnp.exp(scores - row_top), 0.0)
    attn_probs = (weights_raw / lax.optimization_barrier(jnp.sum(weights_raw, axis=-1, keepdims=True))).astype(jnp.bfloat16)
    mixed = jnp.einsum('hgqk,khd->qhgd', attn_probs.astype(jnp.float32), value_heads.astype(jnp.float32))
    return mixed.reshape(seq_len, -1).astype(jnp.bfloat16)

def reference(train_weights, section_layers, prompt_embeds, prompt_lengths):
    offsets = (jnp.cumsum(section_layers) - section_layers).astype(jnp.int32)
    query_cols = QH * HD // N_TP
    kv_cols = KVH * HD // N_TP
    hidden = prompt_embeds
    section_list = []
    cache_list = []
    for section_rank in range(N_SECTION):
        layer_block = lax.dynamic_index_in_dim(train_weights, offsets[section_rank], 0, keepdims=False).reshape(D, N_TP, UNIT)
        w_query = layer_block[:, :, :query_cols].reshape(D, QH * HD)
        w_key = layer_block[:, :, query_cols:query_cols + kv_cols].reshape(D, KVH * HD)
        w_value = layer_block[:, :, query_cols + kv_cols:query_cols + 2 * kv_cols].reshape(D, KVH * HD)
        w_output = layer_block[:, :, query_cols + 2 * kv_cols:]
        normed = rms_rows(hidden).reshape(BATCH * SEQ, D)
        queries = jnp.dot(normed, w_query, preferred_element_type=jnp.float32).reshape(BATCH, SEQ, QH, HD)
        queries = jax.vmap(rotate)(queries).astype(jnp.bfloat16)
        key_heads = jnp.dot(normed, w_key, preferred_element_type=jnp.float32).reshape(BATCH, SEQ, KVH, HD)
        key_heads = jax.vmap(rotate)(key_heads).astype(jnp.bfloat16)
        value_heads = jnp.dot(normed, w_value, preferred_element_type=jnp.float32).reshape(BATCH, SEQ, KVH, HD).astype(jnp.bfloat16)
        attended = jax.vmap(attend)(queries, key_heads, value_heads, prompt_lengths).reshape(BATCH * SEQ, QH * HD)
        total_sum = jnp.zeros((BATCH * SEQ, D), jnp.float32)
        for tp_rank in range(N_TP):
            part_term = lax.dot_general(attended[:, tp_rank * query_cols:(tp_rank + 1) * query_cols], w_output[:, tp_rank, :], (((1,), (1,)), ((), ())), preferred_element_type=jnp.float32)
            rounded = lax.optimization_barrier(part_term.astype(jnp.bfloat16))
            total_sum = total_sum + rounded.astype(jnp.float32)
        hidden = (hidden.astype(jnp.float32) + total_sum.reshape(BATCH, SEQ, D)).astype(jnp.bfloat16)
        section_list.append(hidden)
        cache_list.append(jnp.stack([key_heads.reshape(BATCH, SEQ, KVH * HD), value_heads.reshape(BATCH, SEQ, KVH * HD)], axis=2))
    return (jnp.stack(section_list), jnp.stack(cache_list))
```

```python
import jax
import jax.numpy as jnp
from jax import lax
from jax.sharding import PartitionSpec as P

QH = 32
KVH = 8
HD = 128
ROPE_BASE = 1000000.0
EPS = 1e-06
BF = jnp.bfloat16
F32 = jnp.float32
ORDER = (0, -1, 1, -2, 2, -3, 3, 4)


def shift(value, axis, by):
    n = lax.axis_size(axis)
    return lax.ppermute(value, axis, [(i, (i + by) % n) for i in range(n)])


def swap_core(value):
    n = lax.axis_size("tp")
    return lax.ppermute(value, "tp", [(i, i ^ 1) for i in range(n)])


def ring(block):
    half = block.shape[0] // 2
    a, b = shift(block, "fsdp", 1), shift(block, "fsdp", -1)
    c, d = shift(a, "fsdp", 1), shift(b, "fsdp", -1)
    e, g = shift(c, "fsdp", 1), shift(d, "fsdp", -1)
    i, j = shift(e[:half], "fsdp", 1), shift(g[half:], "fsdp", -1)
    return jnp.concatenate([block, a, b, c, d, e, g, i, j], axis=0)


def rotate(vals, cosine, sine):
    half = vals.shape[-1] // 2
    front, back = vals[..., :half], vals[..., half:]
    return jnp.concatenate([front * cosine - back * sine, back * cosine + front * sine], axis=-1)


def attend(queries, keys, values, length):
    seq = queries.shape[0]
    scores = jnp.einsum("qgd,kd->gqk", queries, keys, preferred_element_type=F32) * HD ** (-0.5)
    row = jnp.arange(seq)[:, None]
    col = jnp.arange(seq)[None, :]
    allowed = (col <= row) & (col < length)
    scores = jnp.where(allowed, scores, -1e30)
    top = jnp.max(scores, axis=-1, keepdims=True)
    raw = jnp.where(allowed, jnp.exp(scores - top), 0.0)
    probs = (raw / jnp.sum(raw, axis=-1, keepdims=True)).astype(BF)
    mixed = jnp.einsum("gqk,kd->qgd", probs, values, preferred_element_type=F32)
    return mixed.reshape(seq, -1).astype(BF)


def shards(train_weights, section_layers, prompt_embeds, prompt_lengths):
    n_fsdp = lax.axis_size("fsdp")
    n_section = lax.axis_size("section")
    n_tp = lax.axis_size("tp")
    f = lax.axis_index("fsdp")
    s = lax.axis_index("section")
    t = lax.axis_index("tp")
    core = t % 2
    rows = train_weights.shape[1]
    prompts, seq, width = prompt_embeds.shape
    tokens = prompts * seq
    q_cols = QH * HD // n_tp
    kv_cols = KVH * HD // n_tp
    qkv_cols = q_cols + 2 * kv_cols
    feats = rows * n_fsdp
    half = feats // 2

    offsets = jnp.cumsum(section_layers) - section_layers
    w_qkv, w_out = [], []
    for layer in range(n_section):
        own = lax.dynamic_index_in_dim(train_weights, offsets[layer], 0, keepdims=False)
        w_qkv.append(ring(own[:, :qkv_cols]))
        w_out.append(ring(own[:, qkv_cols:]))

    flat = prompt_embeds.reshape(tokens, width)
    x = jnp.concatenate(
        [
            lax.dynamic_slice_in_dim(flat, (((f + o) % n_fsdp) * n_section + s) * rows, rows, 1)
            for o in ORDER
        ],
        axis=1,
    )
    half_dim = HD // 2
    frequency = ROPE_BASE ** (-2.0 * jnp.arange(half_dim, dtype=F32) / HD)
    angles = jnp.arange(seq, dtype=F32)[:, None] * frequency[None, :]
    cosine = jnp.cos(angles)[None, :, None, :]
    sine = jnp.sin(angles)[None, :, None, :]

    states, caches = [], []
    for layer in range(n_section):
        part = jnp.dot(x, w_qkv[layer], preferred_element_type=F32)
        wide = x.astype(F32)
        squares = jnp.sum(wide * wide, axis=-1, keepdims=True)
        high = squares.astype(BF)
        low = (squares - high.astype(F32)).astype(BF)
        payload = jnp.concatenate(
            [part.astype(BF), jnp.broadcast_to(high, (tokens, 64)), jnp.broadcast_to(low, (tokens, 64))],
            axis=1,
        )
        got = [shift(payload, "section", k) for k in range(1, n_section)]
        total = part
        for r in got:
            total = total + r[:, :qkv_cols].astype(F32)
            squares = squares + r[:, qkv_cols : qkv_cols + 1].astype(F32)
            squares = squares + r[:, qkv_cols + 64 : qkv_cols + 65].astype(F32)
        qkv = total * lax.rsqrt(squares / width + EPS)
        q = rotate(qkv[:, :q_cols].reshape(prompts, seq, -1, HD), cosine, sine).astype(BF)
        k = rotate(qkv[:, q_cols : q_cols + kv_cols].reshape(prompts, seq, 1, HD), cosine, sine)
        k = k.astype(BF).reshape(prompts, seq, kv_cols)
        v = qkv[:, q_cols + kv_cols :].astype(BF).reshape(prompts, seq, kv_cols)
        mixed = jax.vmap(attend)(q, k, v, prompt_lengths).reshape(tokens, q_cols)
        caches.append(jnp.stack([k, v], axis=2))
        heads = lax.dot_general(
            mixed, w_out[layer], (((1,), (1,)), ((), ())), preferred_element_type=F32
        )
        mine = lax.dynamic_slice_in_dim(heads, core * half, half, 1)
        other = lax.dynamic_slice_in_dim(heads, (1 - core) * half, half, 1).astype(BF)
        mine = mine + swap_core(other).astype(F32)
        sent = mine.astype(BF)
        got = [shift(sent, "tp", 2 * k) for k in range(1, n_tp // 2)]
        for r in got:
            mine = mine + r.astype(F32)
        x_mine = (lax.dynamic_slice_in_dim(x, core * half, half, 1).astype(F32) + mine).astype(BF)
        x_other = swap_core(x_mine)
        x = jnp.where(
            core == 0,
            jnp.concatenate([x_mine, x_other], axis=1),
            jnp.concatenate([x_other, x_mine], axis=1),
        )
        states.append(x)

    kv_out = caches[0]
    for layer in range(1, n_section):
        kv_out = jnp.where(s == layer, caches[layer], kv_out)

    share = seq // n_tp
    stacked = jnp.stack(states).reshape(n_section, prompts, seq, feats)
    stacked = lax.dynamic_slice_in_dim(stacked, t * share, share, 2)
    stacked = stacked.reshape(n_section, prompts * share, feats)
    pieces = []
    for m in range(n_section):
        k = (n_section - m) % n_section
        piece = lax.dynamic_index_in_dim(stacked, (s + k) % n_section, 0, keepdims=False)
        pieces.append(shift(piece, "section", k) if k else piece)
    pieces = jnp.stack(pieces).reshape(n_section, prompts * share, n_fsdp, rows)
    slot = {o % n_fsdp: i for i, o in enumerate(ORDER)}
    pieces = jnp.stack([pieces[:, :, slot[o]] for o in range(n_fsdp)], axis=0)
    pieces = lax.dynamic_slice_in_dim(
        jnp.concatenate([pieces, pieces], axis=0), (n_fsdp - f) % n_fsdp, n_fsdp, 0
    )
    pieces = lax.dynamic_slice_in_dim(
        jnp.concatenate([pieces, pieces], axis=1), (n_section - s) % n_section, n_section, 1
    )
    out = pieces.transpose(2, 0, 1, 3).reshape(1, prompts, share, width)
    return out, kv_out[None]


def solution(mesh):
    in_specs = (P(None, ("fsdp", "section"), "tp"), P(), P("fsdp", None, None), P("fsdp"))
    out_specs = (P("section", "fsdp", "tp", None), P("section", "fsdp", None, None, "tp"))
    return jax.shard_map(shards, mesh=mesh, in_specs=in_specs, out_specs=out_specs, check_vma=False)
```

```python
import jax
import jax.numpy as jnp
from jax import lax
from jax.experimental import pallas as pl
from jax.experimental.pallas import tpu as pltpu
from jax.sharding import PartitionSpec as P

QH = 32
KVH = 8
HD = 128
ROPE_BASE = 1000000.0
EPS = 1e-06
BF = jnp.bfloat16
F32 = jnp.float32
VMEM_LIMIT = 16 * 1024 * 1024
ORDER = ((0, 0), (-1, 0), (1, 0), (-2, 0), (2, 0), (-3, 0), (3, 0), (4, 0), (4, 1))
ANY = pl.BlockSpec(memory_space=pl.ANY)
VMEM = pl.BlockSpec(memory_space=pltpu.VMEM)
SMEM = pl.BlockSpec(memory_space=pltpu.SMEM)


def shift(value, axis, by):
    n = lax.axis_size(axis)
    return lax.ppermute(value, axis, [(i, (i + by) % n) for i in range(n)])


def swap_core(value):
    n = lax.axis_size("tp")
    return lax.ppermute(value, "tp", [(i, i ^ 1) for i in range(n)])


def in_hbm(value):
    return pltpu.with_memory_space_constraint(value, pltpu.HBM)


def after(value, *others):
    return lax.optimization_barrier((value,) + others)[0]


class Ring:
    def __init__(self, block):
        self.half = block.shape[0] // 2
        self.got = [block]

    def step(self, *others):
        k = len(self.got) // 2
        up, down = (self.got[0], self.got[0]) if k == 0 else self.got[-2:]
        if k == 3:
            up, down = up[: self.half], down[self.half :]
        if others:
            up, down = after(up, *others), after(down, *others)
        pair = lax.optimization_barrier((shift(up, "fsdp", 1), shift(down, "fsdp", -1)))
        self.got += pair
        return pair


def call(body, out, in_specs, out_specs, scratch, flops, nbytes, name):
    return pl.pallas_call(
        body,
        out_shape=out,
        in_specs=in_specs,
        out_specs=out_specs,
        scratch_shapes=scratch,
        compiler_params=pltpu.CompilerParams(vmem_limit_bytes=VMEM_LIMIT),
        cost_estimate=pl.CostEstimate(flops=flops, bytes_accessed=nbytes, transcendentals=0),
        name=name,
    )


def pick(train_weights, section_layers, n_section, wanted):
    layers, rows, _ = train_weights.shape
    flat = [
        (out, at, layer, c0, c1)
        for out, (chosen, c0, c1) in enumerate(wanted)
        for at, layer in enumerate(chosen)
    ]

    def body(layers_ref, w_ref, *refs):
        outs, sems = refs[: len(wanted)], refs[len(wanted)]
        offsets = [jnp.int32(0)]
        for layer in range(n_section - 1):
            offsets.append(offsets[-1] + layers_ref[layer])
        copies = [
            pltpu.make_async_copy(
                w_ref.at[jnp.clip(offsets[layer], 0, layers - 1), :, pl.ds(c0, c1 - c0)],
                outs[out].at[pl.ds(at * rows, rows)],
                sems.at[i],
            )
            for i, (out, at, layer, c0, c1) in enumerate(flat)
        ]
        for c in copies:
            c.start()
        for c in copies:
            c.wait()

    return call(
        body,
        tuple(jax.ShapeDtypeStruct((len(chosen) * rows, c1 - c0), BF) for chosen, c0, c1 in wanted),
        [SMEM, ANY],
        (VMEM,) * len(wanted),
        [pltpu.SemaphoreType.DMA((len(flat),))],
        0,
        4 * rows * sum(c1 - c0 for *_, c0, c1 in flat),
        "pick",
    )(section_layers, in_hbm(train_weights))


def ring_copies(f, parts, c0, c1, dst, d0, sems, base):
    rows = parts[0].shape[0]
    n = 8
    copies = []
    for i, (distance, part) in enumerate(ORDER):
        size = parts[i].shape[0]
        at = pl.multiple_of(lax.rem(f + (distance + n), n) * rows + part * size, 16)
        copies.append(
            pltpu.make_async_copy(
                parts[i].at[:, pl.ds(c0, c1 - c0)],
                dst.at[pl.ds(at, size), pl.ds(d0, c1 - c0)],
                sems.at[base + i],
            )
        )
    return copies


def join(place, parts):
    count = len(parts)
    total, cols = 8 * parts[0].shape[0], parts[0].shape[1]

    def body(place_ref, *refs):
        ins, out, sems = refs[:count], refs[count], refs[count + 1]
        copies = ring_copies(place_ref[0], ins, 0, cols, out, 0, sems, 0)
        for c in copies:
            c.start()
        for c in copies:
            c.wait()

    return call(
        body,
        jax.ShapeDtypeStruct((total, cols), BF),
        [SMEM] + [ANY] * count,
        VMEM,
        [pltpu.SemaphoreType.DMA((count,))],
        0,
        4 * total * cols,
        "join",
    )(place, *[in_hbm(p) for p in parts])


def square_lanes(x):
    wide = x.astype(F32)
    squares = jnp.sum(wide * wide, axis=-1, keepdims=True)
    high = squares.astype(BF).astype(F32)
    lane = lax.broadcasted_iota(jnp.int32, (x.shape[0], 128), 1)
    return jnp.where(lane < 64, high, squares - high).astype(BF)


def first_project(x, place, parts):
    tokens, feats = x.shape
    half = tokens // 2
    count, cols = len(parts), parts[0].shape[1]

    def body(place_ref, x_ref, *refs):
        ins = refs[:count]
        mine_ref, other_ref, sq_ref, w, sems = refs[count:]
        copies = ring_copies(place_ref[0], ins, 0, cols, w, 0, sems, 0)
        for c in copies:
            c.start()
        mine_first = place_ref[1] == 0
        top, bottom = x_ref[:half], x_ref[half:]
        mine = jnp.where(mine_first, top, bottom)
        other = jnp.where(mine_first, bottom, top)
        sq_ref[...] = square_lanes(mine)
        for c in copies:
            c.wait()
        both = jnp.dot(jnp.concatenate([mine, other], axis=0), w[...], preferred_element_type=F32)
        mine_ref[...] = both[:half].astype(BF)
        other_ref[...] = both[half:].astype(BF)

    return call(
        body,
        (
            jax.ShapeDtypeStruct((half, cols), BF),
            jax.ShapeDtypeStruct((half, cols), BF),
            jax.ShapeDtypeStruct((half, 128), BF),
        ),
        [SMEM, VMEM] + [ANY] * count,
        (VMEM, VMEM, VMEM),
        [pltpu.VMEM((feats, cols), BF), pltpu.SemaphoreType.DMA((count,))],
        2 * tokens * feats * cols,
        2 * feats * cols,
        "first_project",
    )(place, x, *[in_hbm(p) for p in parts])


def project(x, terms, weights, slot, cols):
    tokens, feats = x.shape
    n = len(terms)
    blocks, cores, _, rows, _ = weights.shape

    def body(x_ref, *refs):
        term_refs = refs[:n]
        w_ref, new_ref, pay_ref, w, sems = refs[n:]
        copies = [
            pltpu.make_async_copy(w_ref.at[:, i, slot, :, pl.ds(0, cols)], w.at[i], sems.at[i])
            for i in range(cores)
        ]
        for c in copies:
            c.start()
        total = x_ref[...].astype(F32)
        for r in term_refs:
            total = total + r[...].astype(F32)
        new = total.astype(BF)
        new_ref[...] = new
        pay_ref[:, 2 * cols :] = square_lanes(new)
        for i, c in enumerate(copies):
            c.wait()
            pay_ref[:, i * cols : (i + 1) * cols] = jnp.dot(
                new, w[i].reshape(feats, cols), preferred_element_type=F32
            ).astype(BF)

    return call(
        body,
        (
            jax.ShapeDtypeStruct((tokens, feats), BF),
            jax.ShapeDtypeStruct((tokens, cores * cols + 128), BF),
        ),
        [VMEM] * (n + 1) + [ANY],
        (VMEM, VMEM),
        [pltpu.VMEM((cores, blocks, rows, cols), BF), pltpu.SemaphoreType.DMA((cores,))],
        4 * tokens * feats * cols,
        4 * feats * cols,
        "project",
    )(x, *terms, in_hbm(weights))


def attend(payloads, place, lengths, cos_t, sin_t, weights, slot, first_col, width, q_cols, kv_cols, last):
    n = len(payloads)
    seq = payloads[0].shape[0]
    cores = 2
    if len(weights) == 1:
        blocks, _, _, rows, _ = weights[0].shape
    else:
        blocks, rows = 1, weights[0].shape[0]
    feats = blocks * rows
    n_out = last or 1
    share = seq // n_out
    block = q_cols + 2 * kv_cols
    group = q_cols // HD

    def body(place_ref, len_ref, cos_ref, sin_ref, *refs):
        pays = refs[:n]
        w_refs = refs[n : n + len(weights)]
        outs = refs[n + len(weights) :]
        kv_own_ref, kv_other_ref, w, sems = outs[n_out:][:4]
        if len(weights) == 1:
            sources = [w_refs[0].at[:, i, slot, :, pl.ds(first_col, q_cols)] for i in range(cores)]
            targets = [w.at[i] for i in range(cores)]
        else:
            sources, targets = w_refs, [w.at[i, 0] for i in range(cores)]
        copies = [
            pltpu.make_async_copy(sources[i], targets[i], sems.at[i]) for i in range(cores)
        ]
        for c in copies:
            c.start()
        total = pays[0][...].astype(F32)
        for r in pays[1:]:
            total = total + r[...].astype(F32)
        squares = total[:, 2 * block : 2 * block + 1] + total[:, 2 * block + 64 : 2 * block + 65]
        factor = lax.rsqrt(squares / width + EPS)
        cos, sin = cos_ref[...], sin_ref[...]

        def turned(vals):
            vals = vals * factor
            return (vals * cos + pltpu.roll(vals, HD // 2, 1) * sin).astype(BF)

        row = lax.broadcasted_iota(jnp.int32, (seq, seq), 0)
        col = lax.broadcasted_iota(jnp.int32, (seq, seq), 1)
        allowed = (col <= row) & (col < len_ref[place_ref[1]])
        allowed = jnp.concatenate([allowed] * group, axis=0)
        part = None
        for i, kv_ref in enumerate((kv_own_ref, kv_other_ref)):
            at = i * block
            q = jnp.concatenate(
                [turned(total[:, at + h * HD : at + (h + 1) * HD]) for h in range(group)], axis=0
            )
            at += q_cols
            k = turned(total[:, at : at + kv_cols])
            v = (total[:, at + kv_cols : at + 2 * kv_cols] * factor).astype(BF)
            kv_ref[:, :kv_cols] = k
            kv_ref[:, kv_cols:] = v
            scores = lax.dot_general(
                q, k, (((1,), (1,)), ((), ())), preferred_element_type=F32
            ) * HD ** (-0.5)
            scores = jnp.where(allowed, scores, -1e30)
            top = jnp.max(scores, axis=-1, keepdims=True)
            raw = jnp.where(allowed, jnp.exp(scores - top), 0.0)
            probs = (raw / jnp.sum(raw, axis=-1, keepdims=True)).astype(BF)
            mixed = jnp.dot(probs, v, preferred_element_type=F32).astype(BF)
            mixed = jnp.concatenate([mixed[h * seq : (h + 1) * seq] for h in range(group)], axis=1)
            copies[i].wait()
            out = lax.dot_general(
                mixed, w[i].reshape(feats, q_cols), (((1,), (1,)), ((), ())), preferred_element_type=F32
            )
            part = out if part is None else part + out
        if not last:
            outs[0][...] = part.astype(BF)
            return
        whole = outs[-1]
        whole[...] = part
        for k in range(n_out):
            at = pl.multiple_of(lax.rem(place_ref[2] + k, n_out) * share, 8)
            outs[k][...] = whole[pl.ds(at, share), :].astype(BF)

    return call(
        body,
        (
            *[jax.ShapeDtypeStruct((share, feats), BF)] * n_out,
            jax.ShapeDtypeStruct((seq, 2 * kv_cols), BF),
            jax.ShapeDtypeStruct((seq, 2 * kv_cols), BF),
        ),
        [SMEM, SMEM, VMEM, VMEM] + [VMEM] * n + [ANY] * len(weights),
        (VMEM,) * (n_out + 2),
        [pltpu.VMEM((cores, blocks, rows, q_cols), BF), pltpu.SemaphoreType.DMA((cores,))]
        + ([pltpu.VMEM((seq, feats), F32)] if last else []),
        4 * seq * feats * q_cols,
        4 * feats * q_cols,
        "attend",
    )(place, lengths, cos_t, sin_t, *payloads, *[in_hbm(w) for w in weights])


def residual(x, terms):
    total = x.astype(F32)
    for r in terms:
        total = total + r.astype(F32)
    return total.astype(BF)


def shards(train_weights, section_layers, prompt_embeds, prompt_lengths):
    n_fsdp = lax.axis_size("fsdp")
    n_section = lax.axis_size("section")
    n_tp = lax.axis_size("tp")
    f = lax.axis_index("fsdp")
    s = lax.axis_index("section")
    t = lax.axis_index("tp")
    core = t % 2
    rows = train_weights.shape[1]
    prompts, seq, width = prompt_embeds.shape
    q_cols = QH * HD // n_tp
    kv_cols = KVH * HD // n_tp
    block = q_cols + 2 * kv_cols
    feats = rows * n_fsdp

    place = jnp.stack([f, core, t // 2]).astype(jnp.int32)
    cols = block + q_cols
    calls = [(1, 2), (3,)]
    first_q, first_o, *later = pick(
        train_weights,
        section_layers,
        n_section,
        [((0,), 0, block), ((0,), block, cols)] + [(chosen, 0, cols) for chosen in calls],
    )
    flat = prompt_embeds.reshape(prompts * seq, width)
    x_all = jnp.concatenate(
        [
            lax.dynamic_slice_in_dim(flat, (k * n_section + s) * rows, rows, 1)
            for k in range(n_fsdp)
        ],
        axis=1,
    )
    x = lax.dynamic_slice_in_dim(x_all, core * seq, seq, 0)
    half_dim = HD // 2
    frequency = ROPE_BASE ** (-2.0 * jnp.arange(half_dim, dtype=F32) / HD)
    angles = jnp.arange(seq, dtype=F32)[:, None] * frequency[None, :]
    cosine, sine = jnp.cos(angles), jnp.sin(angles)
    cos_t = jnp.concatenate([cosine, cosine], axis=1)
    sin_t = jnp.concatenate([-sine, sine], axis=1)
    chips = [
        [k * n_tp + y * 2 + c for k in range(n_fsdp) for c in range(2)] for y in range(n_tp // 2)
    ]
    gathered = {}
    for chosen, piece in zip(calls, later):
        got = lax.all_gather(piece, ("fsdp", "tp"), axis=0, tiled=True, axis_index_groups=chips)
        for slot, layer in enumerate(chosen):
            gathered[layer] = (got.reshape(n_fsdp, 2, len(chosen), rows, cols), slot)

    q_ring, o_ring = Ring(first_q), Ring(first_o)
    q1 = q_ring.step()
    o1 = o_ring.step()
    q2 = q_ring.step(x_all)
    o2 = o_ring.step(cos_t, sin_t)
    q3 = q_ring.step(*o1)
    o_ring.step(*q2)
    q_ring.step(*o2)
    o_ring.step(*q3)

    states, caches = [], []
    terms = None
    for layer in range(n_section):
        last = layer + 1 == n_section
        if layer == 0:
            mine, other, squares = first_project(x_all, place, q_ring.got)
            payload = jnp.concatenate([mine, swap_core(other), squares], axis=1)
            o_own = join(place, [after(o_ring.got[0], payload)] + o_ring.got[1:])
            weights, slot = (o_own, swap_core(o_own)), 0
        else:
            weights, slot = gathered[layer]
            x, payload = project(x, terms, weights, slot, block)
            states.append(x)
            weights = (weights,)
        payloads = [payload] + [shift(payload, "section", k) for k in range(1, n_section)]
        *part, kv_first, kv_second = attend(
            payloads, place, prompt_lengths, cos_t, sin_t, weights, slot, block,
            width, q_cols, kv_cols, n_tp // 2 if last else 0,
        )
        if layer == 0:
            caches.append((kv_first, kv_second))
        else:
            caches.append(
                (jnp.where(core == 0, kv_first, kv_second), jnp.where(core == 0, kv_second, kv_first))
            )
        terms = part[:1] + [shift(part[k if last else 0], "tp", 2 * k) for k in range(1, n_tp // 2)]
    chip_share = 2 * seq // n_tp
    final = residual(lax.dynamic_slice_in_dim(x, t // 2 * chip_share, chip_share, 0), terms)

    kv_own, kv_other = caches[0]
    for layer in range(1, n_section):
        kv_own = jnp.where(s == layer, caches[layer][0], kv_own)
        kv_other = jnp.where(s == layer, caches[layer][1], kv_other)
    kv_swapped = swap_core(kv_other)
    kv_out = jnp.where(
        core == 0, jnp.stack([kv_own, kv_swapped]), jnp.stack([kv_swapped, kv_own])
    ).reshape(1, prompts, seq, 2, kv_cols)

    share = seq // n_tp
    keep, give = [], []
    for state in states:
        keep.append(lax.dynamic_slice_in_dim(state, t * share, share, 0))
        give.append(lax.dynamic_slice_in_dim(state, (t + 1 - 2 * core) * share, share, 0))
    keep.append(lax.dynamic_slice_in_dim(final, core * share, share, 0))
    give.append(lax.dynamic_slice_in_dim(final, (1 - core) * share, share, 0))
    keep, got = jnp.stack(keep), swap_core(jnp.stack(give))
    stacked = jnp.where(
        core == 0, jnp.concatenate([keep, got], axis=1), jnp.concatenate([got, keep], axis=1)
    )
    pieces = []
    for m in range(n_section):
        k = (n_section - m) % n_section
        piece = lax.dynamic_index_in_dim(stacked, (s + k) % n_section, 0, keepdims=False)
        pieces.append(shift(piece, "section", k) if k else piece)
    pieces = jnp.stack(pieces + pieces)
    pieces = lax.dynamic_slice_in_dim(pieces, (n_section - s) % n_section, n_section, 0)
    pieces = pieces.reshape(n_section, prompts * share, n_fsdp, rows)
    out = pieces.transpose(1, 2, 0, 3).reshape(1, prompts, share, width)
    return out, kv_out


def solution(mesh):
    in_specs = (P(None, ("fsdp", "section"), "tp"), P(), P("fsdp", None, None), P("fsdp"))
    out_specs = (P("section", "fsdp", "tp", None), P("section", "fsdp", None, None, "tp"))
    return jax.shard_map(shards, mesh=mesh, in_specs=in_specs, out_specs=out_specs, check_vma=False)
```

```python
import jax
import jax.numpy as jnp
from jax import lax
from jax.experimental import pallas as pl
from jax.experimental.pallas import tpu as pltpu
from jax.sharding import PartitionSpec as P

QH = 32
KVH = 8
HD = 128
ROPE_BASE = 1000000.0
EPS = 1e-06
BF = jnp.bfloat16
F32 = jnp.float32
VMEM_LIMIT = 16 * 1024 * 1024
ORDER = ((0, 0), (-1, 0), (1, 0), (-2, 0), (2, 0), (-3, 0), (3, 0), (4, 0), (4, 1))
ANY = pl.BlockSpec(memory_space=pl.ANY)
VMEM = pl.BlockSpec(memory_space=pltpu.VMEM)
SMEM = pl.BlockSpec(memory_space=pltpu.SMEM)


def shift(value, axis, by):
    n = lax.axis_size(axis)
    return lax.ppermute(value, axis, [(i, (i + by) % n) for i in range(n)])


def swap_core(value):
    n = lax.axis_size("tp")
    return lax.ppermute(value, "tp", [(i, i ^ 1) for i in range(n)])


def in_hbm(value):
    return pltpu.with_memory_space_constraint(value, pltpu.HBM)


def after(value, *others):
    return lax.optimization_barrier((value,) + others)[0]


class Ring:
    def __init__(self, block):
        self.half = block.shape[0] // 2
        self.got = [block]

    def step(self, *others):
        k = len(self.got) // 2
        up, down = (self.got[0], self.got[0]) if k == 0 else self.got[-2:]
        if k == 3:
            up, down = up[: self.half], down[self.half :]
        if others:
            up, down = after(up, *others), after(down, *others)
        pair = lax.optimization_barrier((shift(up, "fsdp", 1), shift(down, "fsdp", -1)))
        self.got += pair
        return pair


def call(body, out, in_specs, out_specs, scratch, flops, nbytes, name):
    return pl.pallas_call(
        body,
        out_shape=out,
        in_specs=in_specs,
        out_specs=out_specs,
        scratch_shapes=scratch,
        compiler_params=pltpu.CompilerParams(vmem_limit_bytes=VMEM_LIMIT),
        cost_estimate=pl.CostEstimate(flops=flops, bytes_accessed=nbytes, transcendentals=0),
        name=name,
    )


def pick(train_weights, section_layers, n_section, wanted):
    layers, rows, _ = train_weights.shape
    flat = [
        (out, at, layer, c0, c1)
        for out, (chosen, c0, c1) in enumerate(wanted)
        for at, layer in enumerate(chosen)
    ]

    def body(layers_ref, w_ref, *refs):
        outs, sems = refs[: len(wanted)], refs[len(wanted)]
        offsets = [jnp.int32(0)]
        for layer in range(n_section - 1):
            offsets.append(offsets[-1] + layers_ref[layer])
        copies = [
            pltpu.make_async_copy(
                w_ref.at[jnp.clip(offsets[layer], 0, layers - 1), :, pl.ds(c0, c1 - c0)],
                outs[out].at[pl.ds(at * rows, rows)],
                sems.at[i],
            )
            for i, (out, at, layer, c0, c1) in enumerate(flat)
        ]
        for c in copies:
            c.start()
        for c in copies:
            c.wait()

    return call(
        body,
        tuple(jax.ShapeDtypeStruct((len(chosen) * rows, c1 - c0), BF) for chosen, c0, c1 in wanted),
        [SMEM, ANY],
        (VMEM,) * len(wanted),
        [pltpu.SemaphoreType.DMA((len(flat),))],
        0,
        4 * rows * sum(c1 - c0 for *_, c0, c1 in flat),
        "pick",
    )(section_layers, in_hbm(train_weights))


def ring_copies(f, parts, c0, c1, dst, d0, sems, base):
    rows = parts[0].shape[0]
    n = 8
    copies = []
    for i, (distance, part) in enumerate(ORDER):
        size = parts[i].shape[0]
        at = pl.multiple_of(lax.rem(f + (distance + n), n) * rows + part * size, 16)
        copies.append(
            pltpu.make_async_copy(
                parts[i].at[:, pl.ds(c0, c1 - c0)],
                dst.at[pl.ds(at, size), pl.ds(d0, c1 - c0)],
                sems.at[base + i],
            )
        )
    return copies


def join(place, parts):
    count = len(parts)
    total, cols = 8 * parts[0].shape[0], parts[0].shape[1]

    def body(place_ref, *refs):
        ins, out, sems = refs[:count], refs[count], refs[count + 1]
        copies = ring_copies(place_ref[0], ins, 0, cols, out, 0, sems, 0)
        for c in copies:
            c.start()
        for c in copies:
            c.wait()

    return call(
        body,
        jax.ShapeDtypeStruct((total, cols), BF),
        [SMEM] + [ANY] * count,
        VMEM,
        [pltpu.SemaphoreType.DMA((count,))],
        0,
        4 * total * cols,
        "join",
    )(place, *[in_hbm(p) for p in parts])


def square_lanes(x):
    wide = x.astype(F32)
    squares = jnp.sum(wide * wide, axis=-1, keepdims=True)
    high = squares.astype(BF).astype(F32)
    lane = lax.broadcasted_iota(jnp.int32, (x.shape[0], 128), 1)
    return jnp.where(lane < 64, high, squares - high).astype(BF)


def first_project(x, place, parts):
    tokens, feats = x.shape
    half = tokens // 2
    count, cols = len(parts), parts[0].shape[1]

    def body(place_ref, x_ref, *refs):
        ins = refs[:count]
        mine_ref, other_ref, sq_ref, w, sems = refs[count:]
        copies = ring_copies(place_ref[0], ins, 0, cols, w, 0, sems, 0)
        for c in copies:
            c.start()
        mine_first = place_ref[1] == 0
        top, bottom = x_ref[:half], x_ref[half:]
        mine = jnp.where(mine_first, top, bottom)
        other = jnp.where(mine_first, bottom, top)
        sq_ref[...] = square_lanes(mine)
        for c in copies:
            c.wait()
        both = jnp.dot(jnp.concatenate([mine, other], axis=0), w[...], preferred_element_type=F32)
        mine_ref[...] = both[:half].astype(BF)
        other_ref[...] = both[half:].astype(BF)

    return call(
        body,
        (
            jax.ShapeDtypeStruct((half, cols), BF),
            jax.ShapeDtypeStruct((half, cols), BF),
            jax.ShapeDtypeStruct((half, 128), BF),
        ),
        [SMEM, VMEM] + [ANY] * count,
        (VMEM, VMEM, VMEM),
        [pltpu.VMEM((feats, cols), BF), pltpu.SemaphoreType.DMA((count,))],
        2 * tokens * feats * cols,
        2 * feats * cols,
        "first_project",
    )(place, x, *[in_hbm(p) for p in parts])


def bring(weights, slot, first, cols):
    blocks, cores, _, rows, _ = weights.shape

    def body(w_ref, out, sems):
        copies = [
            pltpu.make_async_copy(w_ref.at[:, i, slot, :, pl.ds(first, cols)], out.at[i], sems.at[i])
            for i in range(cores)
        ]
        for c in copies:
            c.start()
        for c in copies:
            c.wait()

    size = cores * blocks * rows * cols
    return call(
        body,
        pltpu.VMEM((cores, blocks, rows, cols), BF),
        [ANY],
        VMEM,
        [pltpu.SemaphoreType.DMA((cores,))],
        0,
        4 * size,
        "bring",
    )(in_hbm(weights))


def project(x, terms, weights, slot=None, cols=None):
    tokens, feats = x.shape
    n = len(terms)
    inside = slot is not None
    if inside:
        blocks, cores, _, rows, _ = weights.shape
        weights = in_hbm(weights)
    else:
        cores, blocks, rows, cols = weights.shape

    def body(x_ref, *refs):
        term_refs = refs[:n]
        w, new_ref, pay_ref = refs[n : n + 3]
        copies = []
        if inside:
            source, (w, sems) = w, refs[n + 3 :]
            copies = [
                pltpu.make_async_copy(source.at[:, i, slot, :, pl.ds(0, cols)], w.at[i], sems.at[i])
                for i in range(cores)
            ]
        for c in copies:
            c.start()
        total = x_ref[...].astype(F32)
        for r in term_refs:
            total = total + r[...].astype(F32)
        new = total.astype(BF)
        new_ref[...] = new
        pay_ref[:, cores * cols :] = square_lanes(new)
        for i in range(cores):
            for c in copies[i : i + 1]:
                c.wait()
            pay_ref[:, i * cols : (i + 1) * cols] = jnp.dot(
                new, w[i].reshape(feats, cols), preferred_element_type=F32
            ).astype(BF)

    return call(
        body,
        (
            jax.ShapeDtypeStruct((tokens, feats), BF),
            jax.ShapeDtypeStruct((tokens, cores * cols + 128), BF),
        ),
        [VMEM] * (n + 1) + [ANY if inside else VMEM],
        (VMEM, VMEM),
        [pltpu.VMEM((cores, blocks, rows, cols), BF), pltpu.SemaphoreType.DMA((cores,))]
        if inside
        else [],
        4 * tokens * feats * cols,
        4 * feats * cols,
        "project",
    )(x, *terms, weights)


def attend(payloads, place, lengths, cos_t, sin_t, weights, width, q_cols, kv_cols, last):
    n = len(payloads)
    seq = payloads[0].shape[0]
    n_in = len(weights)
    feats = weights[0].size // (q_cols * (2 // n_in))
    n_out = last or 1
    share = seq // n_out
    block = q_cols + 2 * kv_cols
    group = q_cols // HD

    def body(place_ref, len_ref, cos_ref, sin_ref, *refs):
        pays, w_refs, outs = refs[:n], refs[n : n + n_in], refs[n + n_in :]
        kv_refs = outs[n_out : n_out + 2]
        total = pays[0][...].astype(F32)
        for r in pays[1:]:
            total = total + r[...].astype(F32)
        squares = total[:, 2 * block : 2 * block + 1] + total[:, 2 * block + 64 : 2 * block + 65]
        factor = lax.rsqrt(squares / width + EPS)
        cos, sin = cos_ref[...] * factor, sin_ref[...] * factor

        def turned(vals):
            return (vals * cos + pltpu.roll(vals, HD // 2, 1) * sin).astype(BF)

        row = lax.broadcasted_iota(jnp.int32, (seq, seq), 0)
        col = lax.broadcasted_iota(jnp.int32, (seq, seq), 1)
        allowed = (col <= row) & (col < len_ref[place_ref[1]])
        allowed = jnp.concatenate([allowed] * group, axis=0)
        mixed = []
        for i, kv_ref in enumerate(kv_refs):
            at = i * block
            q = jnp.concatenate(
                [turned(total[:, at + h * HD : at + (h + 1) * HD]) for h in range(group)], axis=0
            )
            at += q_cols
            k = turned(total[:, at : at + kv_cols])
            v = (total[:, at + kv_cols : at + 2 * kv_cols] * factor).astype(BF)
            kv_ref[:, :kv_cols] = k
            kv_ref[:, kv_cols:] = v
            scores = lax.dot_general(
                q, k, (((1,), (1,)), ((), ())), preferred_element_type=F32
            ) * HD ** (-0.5)
            scores = jnp.where(allowed, scores, -1e30)
            top = jnp.max(scores, axis=-1, keepdims=True)
            raw = jnp.where(allowed, jnp.exp(scores - top), 0.0)
            probs = (raw / jnp.sum(raw, axis=-1, keepdims=True)).astype(BF)
            out = jnp.dot(probs, v, preferred_element_type=F32).astype(BF)
            mixed.append(
                jnp.concatenate([out[h * seq : (h + 1) * seq] for h in range(group)], axis=1)
            )
        part = None
        for i in range(2):
            w = w_refs[i][...] if n_in == 2 else w_refs[0][i]
            out = lax.dot_general(
                mixed[i], w.reshape(feats, q_cols), (((1,), (1,)), ((), ())),
                preferred_element_type=F32,
            )
            part = out if part is None else part + out
        if not last:
            outs[0][...] = part.astype(BF)
            return
        whole = outs[-1]
        whole[...] = part
        for k in range(n_out):
            at = pl.multiple_of(lax.rem(place_ref[2] + k, n_out) * share, 8)
            outs[k][...] = whole[pl.ds(at, share), :].astype(BF)

    return call(
        body,
        (
            *[jax.ShapeDtypeStruct((share, feats), BF)] * n_out,
            jax.ShapeDtypeStruct((seq, 2 * kv_cols), BF),
            jax.ShapeDtypeStruct((seq, 2 * kv_cols), BF),
        ),
        [SMEM, SMEM, VMEM, VMEM] + [VMEM] * (n + n_in),
        (VMEM,) * (n_out + 2),
        [pltpu.VMEM((seq, feats), F32)] if last else [],
        4 * seq * feats * q_cols,
        4 * feats * q_cols,
        "attend",
    )(place, lengths, cos_t, sin_t, *payloads, *weights)


def residual(x, terms):
    total = x.astype(F32)
    for r in terms:
        total = total + r.astype(F32)
    return total.astype(BF)


def shards(train_weights, section_layers, prompt_embeds, prompt_lengths):
    n_fsdp = lax.axis_size("fsdp")
    n_section = lax.axis_size("section")
    n_tp = lax.axis_size("tp")
    f = lax.axis_index("fsdp")
    s = lax.axis_index("section")
    t = lax.axis_index("tp")
    core = t % 2
    rows = train_weights.shape[1]
    prompts, seq, width = prompt_embeds.shape
    q_cols = QH * HD // n_tp
    kv_cols = KVH * HD // n_tp
    block = q_cols + 2 * kv_cols
    feats = rows * n_fsdp

    place = jnp.stack([f, core, t // 2]).astype(jnp.int32)
    cols = block + q_cols
    calls = [(1, 2), (3,)]
    first_q, first_o, *later = pick(
        train_weights,
        section_layers,
        n_section,
        [((0,), 0, block), ((0,), block, cols)] + [(chosen, 0, cols) for chosen in calls],
    )
    flat = prompt_embeds.reshape(prompts * seq, width)
    x_all = jnp.concatenate(
        [
            lax.dynamic_slice_in_dim(flat, (k * n_section + s) * rows, rows, 1)
            for k in range(n_fsdp)
        ],
        axis=1,
    )
    x = lax.dynamic_slice_in_dim(x_all, core * seq, seq, 0)
    half_dim = HD // 2
    frequency = ROPE_BASE ** (-2.0 * jnp.arange(half_dim, dtype=F32) / HD)
    angles = jnp.arange(seq, dtype=F32)[:, None] * frequency[None, :]
    cosine, sine = jnp.cos(angles), jnp.sin(angles)
    cos_t = jnp.concatenate([cosine, cosine], axis=1)
    sin_t = jnp.concatenate([-sine, sine], axis=1)
    chips = [
        [k * n_tp + y * 2 + c for k in range(n_fsdp) for c in range(2)] for y in range(n_tp // 2)
    ]
    gathered = {}
    for chosen, piece in zip(calls, later):
        got = lax.all_gather(piece, ("fsdp", "tp"), axis=0, tiled=True, axis_index_groups=chips)
        for slot, layer in enumerate(chosen):
            gathered[layer] = (got.reshape(n_fsdp, 2, len(chosen), rows, cols), slot)

    q_ring, o_ring = Ring(first_q), Ring(first_o)
    q1 = q_ring.step()
    o1 = o_ring.step()
    q2 = q_ring.step(x_all)
    o2 = o_ring.step(cos_t, sin_t)
    q3 = q_ring.step(*o1)
    o_ring.step(*q2)
    q_ring.step(*o2)
    o_ring.step(*q3)

    states, caches = [], []
    terms = None
    for layer in range(n_section):
        last = layer + 1 == n_section
        if layer == 0:
            mine, other, squares = first_project(x_all, place, q_ring.got)
            payload = jnp.concatenate([mine, swap_core(other), squares], axis=1)
            o_own = join(place, [after(o_ring.got[0], payload)] + o_ring.got[1:])
            weights = (o_own, swap_core(o_own))
        else:
            array, slot = gathered[layer]
            if layer == 1:
                x, payload = project(x, terms, array, slot, block)
            else:
                x, payload = project(x, terms, bring(after(array, part[0]), slot, 0, block))
            states.append(x)
            weights = (bring(after(array, payload), slot, block, q_cols),)
        payloads = [payload] + [shift(payload, "section", k) for k in range(1, n_section)]
        *part, kv_first, kv_second = attend(
            payloads, place, prompt_lengths, cos_t, sin_t, weights,
            width, q_cols, kv_cols, n_tp // 2 if last else 0,
        )
        if layer == 0:
            caches.append((kv_first, kv_second))
        else:
            caches.append(
                (jnp.where(core == 0, kv_first, kv_second), jnp.where(core == 0, kv_second, kv_first))
            )
        terms = part[:1] + [shift(part[k if last else 0], "tp", 2 * k) for k in range(1, n_tp // 2)]
    chip_share = 2 * seq // n_tp
    final = residual(lax.dynamic_slice_in_dim(x, t // 2 * chip_share, chip_share, 0), terms)

    kv_own, kv_other = caches[0]
    for layer in range(1, n_section):
        kv_own = jnp.where(s == layer, caches[layer][0], kv_own)
        kv_other = jnp.where(s == layer, caches[layer][1], kv_other)
    kv_swapped = swap_core(kv_other)
    kv_out = jnp.where(
        core == 0, jnp.stack([kv_own, kv_swapped]), jnp.stack([kv_swapped, kv_own])
    ).reshape(1, prompts, seq, 2, kv_cols)

    share = seq // n_tp
    keep, give = [], []
    for state in states:
        keep.append(lax.dynamic_slice_in_dim(state, t * share, share, 0))
        give.append(lax.dynamic_slice_in_dim(state, (t + 1 - 2 * core) * share, share, 0))
    keep.append(lax.dynamic_slice_in_dim(final, core * share, share, 0))
    give.append(lax.dynamic_slice_in_dim(final, (1 - core) * share, share, 0))
    keep, got = jnp.stack(keep), swap_core(jnp.stack(give))
    stacked = jnp.where(
        core == 0, jnp.concatenate([keep, got], axis=1), jnp.concatenate([got, keep], axis=1)
    )
    pieces = []
    for m in range(n_section):
        k = (n_section - m) % n_section
        piece = lax.dynamic_index_in_dim(stacked, (s + k) % n_section, 0, keepdims=False)
        pieces.append(shift(piece, "section", k) if k else piece)
    pieces = jnp.stack(pieces + pieces)
    pieces = lax.dynamic_slice_in_dim(pieces, (n_section - s) % n_section, n_section, 0)
    pieces = pieces.reshape(n_section, prompts * share, n_fsdp, rows)
    out = pieces.transpose(1, 2, 0, 3).reshape(1, prompts, share, width)
    return out, kv_out


def solution(mesh):
    in_specs = (P(None, ("fsdp", "section"), "tp"), P(), P("fsdp", None, None), P("fsdp"))
    out_specs = (P("section", "fsdp", "tp", None), P("section", "fsdp", None, None, "tp"))
    return jax.shard_map(shards, mesh=mesh, in_specs=in_specs, out_specs=out_specs, check_vma=False)
```

```python
import jax
import jax.numpy as jnp
from jax import lax
from jax.experimental import pallas as pl
from jax.experimental.pallas import tpu as pltpu
from jax.sharding import PartitionSpec as P

QH = 32
KVH = 8
HD = 128
ROPE_BASE = 1000000.0
EPS = 1e-06
BF = jnp.bfloat16
F32 = jnp.float32
VMEM_LIMIT = 16 * 1024 * 1024
ORDER = ((0, 0), (-1, 0), (1, 0), (-2, 0), (2, 0), (-3, 0), (3, 0), (4, 0), (4, 1))
ANY = pl.BlockSpec(memory_space=pl.ANY)
VMEM = pl.BlockSpec(memory_space=pltpu.VMEM)
SMEM = pl.BlockSpec(memory_space=pltpu.SMEM)


def shift(value, axis, by):
    n = lax.axis_size(axis)
    return lax.ppermute(value, axis, [(i, (i + by) % n) for i in range(n)])


def swap_core(value):
    n = lax.axis_size("tp")
    return lax.ppermute(value, "tp", [(i, i ^ 1) for i in range(n)])


def in_hbm(value):
    return pltpu.with_memory_space_constraint(value, pltpu.HBM)


def after(value, *others):
    return lax.optimization_barrier((value,) + others)[0]


class Ring:
    def __init__(self, block):
        self.half = block.shape[0] // 2
        self.got = [block]

    def step(self, *others):
        k = len(self.got) // 2
        up, down = (self.got[0], self.got[0]) if k == 0 else self.got[-2:]
        if k == 3:
            up, down = up[: self.half], down[self.half :]
        if others:
            up, down = after(up, *others), after(down, *others)
        pair = lax.optimization_barrier((shift(up, "fsdp", 1), shift(down, "fsdp", -1)))
        self.got += pair
        return pair


def call(body, out, in_specs, out_specs, scratch, flops, nbytes, name):
    return pl.pallas_call(
        body,
        out_shape=out,
        in_specs=in_specs,
        out_specs=out_specs,
        scratch_shapes=scratch,
        compiler_params=pltpu.CompilerParams(vmem_limit_bytes=VMEM_LIMIT),
        cost_estimate=pl.CostEstimate(flops=flops, bytes_accessed=nbytes, transcendentals=0),
        name=name,
    )


def pick(train_weights, section_layers, n_section, wanted):
    layers, rows, _ = train_weights.shape
    flat = [
        (out, at, layer, c0, c1)
        for out, (chosen, c0, c1) in enumerate(wanted)
        for at, layer in enumerate(chosen)
    ]

    def body(layers_ref, w_ref, *refs):
        outs, sems = refs[: len(wanted)], refs[len(wanted)]
        offsets = [jnp.int32(0)]
        for layer in range(n_section - 1):
            offsets.append(offsets[-1] + layers_ref[layer])
        copies = [
            pltpu.make_async_copy(
                w_ref.at[jnp.clip(offsets[layer], 0, layers - 1), :, pl.ds(c0, c1 - c0)],
                outs[out].at[pl.ds(at * rows, rows)],
                sems.at[i],
            )
            for i, (out, at, layer, c0, c1) in enumerate(flat)
        ]
        for c in copies:
            c.start()
        for c in copies:
            c.wait()

    return call(
        body,
        tuple(jax.ShapeDtypeStruct((len(chosen) * rows, c1 - c0), BF) for chosen, c0, c1 in wanted),
        [SMEM, ANY],
        (VMEM,) * len(wanted),
        [pltpu.SemaphoreType.DMA((len(flat),))],
        0,
        4 * rows * sum(c1 - c0 for *_, c0, c1 in flat),
        "pick",
    )(section_layers, in_hbm(train_weights))


def ring_copies(f, parts, c0, c1, dst, d0, sems, base):
    rows = parts[0].shape[0]
    n = 8
    copies = []
    for i, (distance, part) in enumerate(ORDER):
        size = parts[i].shape[0]
        at = pl.multiple_of(lax.rem(f + (distance + n), n) * rows + part * size, 16)
        copies.append(
            pltpu.make_async_copy(
                parts[i].at[:, pl.ds(c0, c1 - c0)],
                dst.at[pl.ds(at, size), pl.ds(d0, c1 - c0)],
                sems.at[base + i],
            )
        )
    return copies


def join(place, parts):
    count = len(parts)
    total, cols = 8 * parts[0].shape[0], parts[0].shape[1]

    def body(place_ref, *refs):
        ins, out, sems = refs[:count], refs[count], refs[count + 1]
        copies = ring_copies(place_ref[0], ins, 0, cols, out, 0, sems, 0)
        for c in copies:
            c.start()
        for c in copies:
            c.wait()

    return call(
        body,
        jax.ShapeDtypeStruct((total, cols), BF),
        [SMEM] + [ANY] * count,
        VMEM,
        [pltpu.SemaphoreType.DMA((count,))],
        0,
        4 * total * cols,
        "join",
    )(place, *[in_hbm(p) for p in parts])


def square_lanes(x):
    wide = x.astype(F32)
    squares = jnp.sum(wide * wide, axis=-1, keepdims=True)
    high = squares.astype(BF).astype(F32)
    lane = lax.broadcasted_iota(jnp.int32, (x.shape[0], 128), 1)
    return jnp.where(lane < 64, high, squares - high).astype(BF)


def first_project(x, place, parts):
    tokens, feats = x.shape
    half = tokens // 2
    count, cols = len(parts), parts[0].shape[1]

    def body(place_ref, x_ref, *refs):
        ins = refs[:count]
        mine_ref, other_ref, sq_ref, w, sems = refs[count:]
        copies = ring_copies(place_ref[0], ins, 0, cols, w, 0, sems, 0)
        for c in copies:
            c.start()
        mine_first = place_ref[1] == 0
        top, bottom = x_ref[:half], x_ref[half:]
        mine = jnp.where(mine_first, top, bottom)
        other = jnp.where(mine_first, bottom, top)
        sq_ref[...] = square_lanes(mine)
        for c in copies:
            c.wait()
        both = jnp.dot(jnp.concatenate([mine, other], axis=0), w[...], preferred_element_type=F32)
        mine_ref[...] = both[:half].astype(BF)
        other_ref[...] = both[half:].astype(BF)

    return call(
        body,
        (
            jax.ShapeDtypeStruct((half, cols), BF),
            jax.ShapeDtypeStruct((half, cols), BF),
            jax.ShapeDtypeStruct((half, 128), BF),
        ),
        [SMEM, VMEM] + [ANY] * count,
        (VMEM, VMEM, VMEM),
        [pltpu.VMEM((feats, cols), BF), pltpu.SemaphoreType.DMA((count,))],
        2 * tokens * feats * cols,
        2 * feats * cols,
        "first_project",
    )(place, x, *[in_hbm(p) for p in parts])


def bring(weights, slot, first, cols):
    blocks, cores, _, rows, _ = weights.shape

    def body(w_ref, out, sems):
        copies = [
            pltpu.make_async_copy(w_ref.at[:, i, slot, :, pl.ds(first, cols)], out.at[i], sems.at[i])
            for i in range(cores)
        ]
        for c in copies:
            c.start()
        for c in copies:
            c.wait()

    size = cores * blocks * rows * cols
    return call(
        body,
        pltpu.VMEM((cores, blocks, rows, cols), BF),
        [ANY],
        VMEM,
        [pltpu.SemaphoreType.DMA((cores,))],
        0,
        4 * size,
        "bring",
    )(in_hbm(weights))


def project(x, terms, weights, slot=None, cols=None):
    tokens, feats = x.shape
    n = len(terms)
    inside = slot is not None
    if inside:
        blocks, cores, _, rows, _ = weights.shape
        weights = in_hbm(weights)
        terms = [in_hbm(r) for r in terms]
    else:
        cores, blocks, rows, cols = weights.shape

    def body(x_ref, *refs):
        term_refs = refs[:n]
        w, new_ref, pay_ref = refs[n : n + 3]
        copies = []
        if inside:
            source, (w, brought, sems) = w, refs[n + 3 :]
            copies = [
                pltpu.make_async_copy(source.at[:, i, slot, :, pl.ds(0, cols)], w.at[i], sems.at[i])
                for i in range(cores)
            ]
            first = [
                pltpu.make_async_copy(r, brought.at[i], sems.at[cores + i])
                for i, r in enumerate(term_refs)
            ]
            for c in first + copies:
                c.start()
            for c in first:
                c.wait()
            term_refs = [brought.at[i] for i in range(n)]
        total = x_ref[...].astype(F32)
        for r in term_refs:
            total = total + r[...].astype(F32)
        new = total.astype(BF)
        new_ref[...] = new
        pay_ref[:, cores * cols :] = square_lanes(new)
        for i in range(cores):
            for c in copies[i : i + 1]:
                c.wait()
            pay_ref[:, i * cols : (i + 1) * cols] = jnp.dot(
                new, w[i].reshape(feats, cols), preferred_element_type=F32
            ).astype(BF)

    return call(
        body,
        (
            jax.ShapeDtypeStruct((tokens, feats), BF),
            jax.ShapeDtypeStruct((tokens, cores * cols + 128), BF),
        ),
        [VMEM] + [ANY if inside else VMEM] * (n + 1),
        (VMEM, VMEM),
        [
            pltpu.VMEM((cores, blocks, rows, cols), BF),
            pltpu.VMEM((n, tokens, feats), BF),
            pltpu.SemaphoreType.DMA((cores + n,)),
        ]
        if inside
        else [],
        4 * tokens * feats * cols,
        4 * feats * cols,
        "project",
    )(x, *terms, weights)


def attend(payloads, place, lengths, cos_t, sin_t, weights, width, q_cols, kv_cols, last):
    n = len(payloads)
    seq = payloads[0].shape[0]
    n_in = len(weights)
    feats = weights[0].size // (q_cols * (2 // n_in))
    n_out = last or 1
    share = seq // n_out
    block = q_cols + 2 * kv_cols
    group = q_cols // HD

    def body(place_ref, len_ref, cos_ref, sin_ref, *refs):
        pays, w_refs, outs = refs[:n], refs[n : n + n_in], refs[n + n_in :]
        kv_refs = outs[n_out : n_out + 2]
        total = pays[0][...].astype(F32)
        for r in pays[1:]:
            total = total + r[...].astype(F32)
        squares = total[:, 2 * block : 2 * block + 1] + total[:, 2 * block + 64 : 2 * block + 65]
        factor = lax.rsqrt(squares / width + EPS)
        cos, sin = cos_ref[...] * factor, sin_ref[...] * factor

        def turned(vals):
            return (vals * cos + pltpu.roll(vals, HD // 2, 1) * sin).astype(BF)

        row = lax.broadcasted_iota(jnp.int32, (seq, seq), 0)
        col = lax.broadcasted_iota(jnp.int32, (seq, seq), 1)
        allowed = (col <= row) & (col < len_ref[place_ref[1]])
        allowed = jnp.concatenate([allowed] * group, axis=0)
        mixed = []
        for i, kv_ref in enumerate(kv_refs):
            at = i * block
            q = jnp.concatenate(
                [turned(total[:, at + h * HD : at + (h + 1) * HD]) for h in range(group)], axis=0
            )
            at += q_cols
            k = turned(total[:, at : at + kv_cols])
            v = (total[:, at + kv_cols : at + 2 * kv_cols] * factor).astype(BF)
            kv_ref[:, :kv_cols] = k
            kv_ref[:, kv_cols:] = v
            scores = lax.dot_general(
                q, k, (((1,), (1,)), ((), ())), preferred_element_type=F32
            ) * HD ** (-0.5)
            scores = jnp.where(allowed, scores, -1e30)
            top = jnp.max(scores, axis=-1, keepdims=True)
            raw = jnp.where(allowed, jnp.exp(scores - top), 0.0)
            probs = (raw / jnp.sum(raw, axis=-1, keepdims=True)).astype(BF)
            out = jnp.dot(probs, v, preferred_element_type=F32).astype(BF)
            mixed.append(
                jnp.concatenate([out[h * seq : (h + 1) * seq] for h in range(group)], axis=1)
            )
        part = None
        for i in range(2):
            w = w_refs[i][...] if n_in == 2 else w_refs[0][i]
            out = lax.dot_general(
                mixed[i], w.reshape(feats, q_cols), (((1,), (1,)), ((), ())),
                preferred_element_type=F32,
            )
            part = out if part is None else part + out
        if not last:
            outs[0][...] = part.astype(BF)
            return
        whole = outs[-1]
        whole[...] = part
        for k in range(n_out):
            at = pl.multiple_of(lax.rem(place_ref[2] + k, n_out) * share, 8)
            outs[k][...] = whole[pl.ds(at, share), :].astype(BF)

    return call(
        body,
        (
            *[jax.ShapeDtypeStruct((share, feats), BF)] * n_out,
            jax.ShapeDtypeStruct((seq, 2 * kv_cols), BF),
            jax.ShapeDtypeStruct((seq, 2 * kv_cols), BF),
        ),
        [SMEM, SMEM, VMEM, VMEM] + [VMEM] * (n + n_in),
        (VMEM,) * (n_out + 2),
        [pltpu.VMEM((seq, feats), F32)] if last else [],
        4 * seq * feats * q_cols,
        4 * feats * q_cols,
        "attend",
    )(place, lengths, cos_t, sin_t, *payloads, *weights)


def residual(x, terms):
    total = x.astype(F32)
    for r in terms:
        total = total + r.astype(F32)
    return total.astype(BF)


def shards(train_weights, section_layers, prompt_embeds, prompt_lengths):
    n_fsdp = lax.axis_size("fsdp")
    n_section = lax.axis_size("section")
    n_tp = lax.axis_size("tp")
    f = lax.axis_index("fsdp")
    s = lax.axis_index("section")
    t = lax.axis_index("tp")
    core = t % 2
    rows = train_weights.shape[1]
    prompts, seq, width = prompt_embeds.shape
    q_cols = QH * HD // n_tp
    kv_cols = KVH * HD // n_tp
    block = q_cols + 2 * kv_cols
    feats = rows * n_fsdp

    place = jnp.stack([f, core, t // 2]).astype(jnp.int32)
    cols = block + q_cols
    calls = [(1, 2), (3,)]
    first_q, first_o, *later = pick(
        train_weights,
        section_layers,
        n_section,
        [((0,), 0, block), ((0,), block, cols)] + [(chosen, 0, cols) for chosen in calls],
    )
    flat = prompt_embeds.reshape(prompts * seq, width)
    x_all = jnp.concatenate(
        [
            lax.dynamic_slice_in_dim(flat, (k * n_section + s) * rows, rows, 1)
            for k in range(n_fsdp)
        ],
        axis=1,
    )
    x = lax.dynamic_slice_in_dim(x_all, core * seq, seq, 0)
    half_dim = HD // 2
    frequency = ROPE_BASE ** (-2.0 * jnp.arange(half_dim, dtype=F32) / HD)
    angles = jnp.arange(seq, dtype=F32)[:, None] * frequency[None, :]
    cosine, sine = jnp.cos(angles), jnp.sin(angles)
    cos_t = jnp.concatenate([cosine, cosine], axis=1)
    sin_t = jnp.concatenate([-sine, sine], axis=1)
    chips = [
        [k * n_tp + y * 2 + c for k in range(n_fsdp) for c in range(2)] for y in range(n_tp // 2)
    ]
    gathered = {}
    for chosen, piece in zip(calls, later):
        got = lax.all_gather(piece, ("fsdp", "tp"), axis=0, tiled=True, axis_index_groups=chips)
        for slot, layer in enumerate(chosen):
            gathered[layer] = (got.reshape(n_fsdp, 2, len(chosen), rows, cols), slot)

    q_ring, o_ring = Ring(first_q), Ring(first_o)
    q1 = q_ring.step()
    o1 = o_ring.step()
    q2 = q_ring.step(x_all)
    o2 = o_ring.step(cos_t, sin_t)
    q3 = q_ring.step(*o1)
    o_ring.step(*q2)
    q_ring.step(*o2)
    o_ring.step(*q3)

    states, caches = [], []
    terms = None
    for layer in range(n_section):
        last = layer + 1 == n_section
        if layer == 0:
            mine, other, squares = first_project(x_all, place, q_ring.got)
            payload = jnp.concatenate([mine, swap_core(other), squares], axis=1)
            o_own = join(place, [after(o_ring.got[0], payload)] + o_ring.got[1:])
            weights = (o_own, swap_core(o_own))
        else:
            array, slot = gathered[layer]
            if layer == 1:
                x, payload = project(x, terms, array, slot, block)
            else:
                x, payload = project(x, terms, bring(after(array, part[0]), slot, 0, block))
            states.append(x)
            weights = (bring(after(array, payload), slot, block, q_cols),)
        payloads = [payload] + [shift(payload, "section", k) for k in (2, 1, 3)]
        *part, kv_first, kv_second = attend(
            payloads, place, prompt_lengths, cos_t, sin_t, weights,
            width, q_cols, kv_cols, n_tp // 2 if last else 0,
        )
        if layer == 0:
            caches.append((kv_first, kv_second))
        else:
            caches.append(
                (jnp.where(core == 0, kv_first, kv_second), jnp.where(core == 0, kv_second, kv_first))
            )
        terms = part[:1] + [shift(part[k if last else 0], "tp", 2 * k) for k in (2, 1, 3)]
    kv_own, kv_other = caches[0]
    for layer in range(1, n_section):
        kv_own = jnp.where(s == layer, caches[layer][0], kv_own)
        kv_other = jnp.where(s == layer, caches[layer][1], kv_other)
    kv_swapped = swap_core(kv_other)
    kv_out = jnp.where(
        core == 0, jnp.stack([kv_own, kv_swapped]), jnp.stack([kv_swapped, kv_own])
    ).reshape(1, prompts, seq, 2, kv_cols)
    terms[0] = after(terms[0], kv_out)
    chip_share = 2 * seq // n_tp
    final = residual(lax.dynamic_slice_in_dim(x, t // 2 * chip_share, chip_share, 0), terms)

    share = seq // n_tp
    keep, give = [], []
    for state in states:
        keep.append(lax.dynamic_slice_in_dim(state, t * share, share, 0))
        give.append(lax.dynamic_slice_in_dim(state, (t + 1 - 2 * core) * share, share, 0))
    keep.append(lax.dynamic_slice_in_dim(final, core * share, share, 0))
    give.append(lax.dynamic_slice_in_dim(final, (1 - core) * share, share, 0))
    keep, got = jnp.stack(keep), swap_core(jnp.stack(give))
    stacked = jnp.where(
        core == 0, jnp.concatenate([keep, got], axis=1), jnp.concatenate([got, keep], axis=1)
    )
    pieces = [None] * n_section
    for k in (2, 1, 3, 0):
        piece = lax.dynamic_index_in_dim(stacked, (s + k) % n_section, 0, keepdims=False)
        pieces[-k % n_section] = shift(piece, "section", k) if k else piece
    pieces = jnp.stack(pieces + pieces)
    pieces = lax.dynamic_slice_in_dim(pieces, (n_section - s) % n_section, n_section, 0)
    pieces = pieces.reshape(n_section, prompts * share, n_fsdp, rows)
    out = pieces.transpose(1, 2, 0, 3).reshape(1, prompts, share, width)
    return out, kv_out


def solution(mesh):
    in_specs = (P(None, ("fsdp", "section"), "tp"), P(), P("fsdp", None, None), P("fsdp"))
    out_specs = (P("section", "fsdp", "tp", None), P("section", "fsdp", None, None, "tp"))
    return jax.shard_map(shards, mesh=mesh, in_specs=in_specs, out_specs=out_specs, check_vma=False)
```

```python
import jax
import jax.numpy as jnp
from jax import lax
from jax.experimental import pallas as pl
from jax.experimental.pallas import tpu as pltpu
from jax.sharding import PartitionSpec as P

QH = 32
KVH = 8
HD = 128
ROPE_BASE = 1000000.0
EPS = 1e-06
BF = jnp.bfloat16
F32 = jnp.float32
VMEM_LIMIT = 16 * 1024 * 1024
ORDER = ((0, 0), (-1, 0), (1, 0), (-2, 0), (2, 0), (-3, 0), (3, 0), (4, 0), (4, 1))
ANY = pl.BlockSpec(memory_space=pl.ANY)
VMEM = pl.BlockSpec(memory_space=pltpu.VMEM)
SMEM = pl.BlockSpec(memory_space=pltpu.SMEM)


def shift(value, axis, by):
    n = lax.axis_size(axis)
    return lax.ppermute(value, axis, [(i, (i + by) % n) for i in range(n)])


def swap_core(value):
    n = lax.axis_size("tp")
    return lax.ppermute(value, "tp", [(i, i ^ 1) for i in range(n)])


def in_hbm(value):
    return pltpu.with_memory_space_constraint(value, pltpu.HBM)


def after(value, *others):
    return lax.optimization_barrier((value,) + others)[0]


class Ring:
    def __init__(self, block):
        self.half = block.shape[0] // 2
        self.got = [block]

    def step(self, *others):
        k = len(self.got) // 2
        up, down = (self.got[0], self.got[0]) if k == 0 else self.got[-2:]
        if k == 3:
            up, down = up[: self.half], down[self.half :]
        if others:
            up, down = after(up, *others), after(down, *others)
        pair = lax.optimization_barrier((shift(up, "fsdp", 1), shift(down, "fsdp", -1)))
        self.got += pair
        return pair


def call(body, out, in_specs, out_specs, scratch, flops, nbytes, name):
    return pl.pallas_call(
        body,
        out_shape=out,
        in_specs=in_specs,
        out_specs=out_specs,
        scratch_shapes=scratch,
        compiler_params=pltpu.CompilerParams(vmem_limit_bytes=VMEM_LIMIT),
        cost_estimate=pl.CostEstimate(flops=flops, bytes_accessed=nbytes, transcendentals=0),
        name=name,
    )


def pick(train_weights, section_layers, n_section, wanted):
    layers, rows, _ = train_weights.shape
    flat = [
        (out, at, layer, c0, c1)
        for out, (chosen, c0, c1) in enumerate(wanted)
        for at, layer in enumerate(chosen)
    ]

    def body(layers_ref, w_ref, *refs):
        outs, sems = refs[: len(wanted)], refs[len(wanted)]
        offsets = [jnp.int32(0)]
        for layer in range(n_section - 1):
            offsets.append(offsets[-1] + layers_ref[layer])
        copies = [
            pltpu.make_async_copy(
                w_ref.at[jnp.clip(offsets[layer], 0, layers - 1), :, pl.ds(c0, c1 - c0)],
                outs[out].at[pl.ds(at * rows, rows)],
                sems.at[i],
            )
            for i, (out, at, layer, c0, c1) in enumerate(flat)
        ]
        for c in copies:
            c.start()
        for c in copies:
            c.wait()

    return call(
        body,
        tuple(jax.ShapeDtypeStruct((len(chosen) * rows, c1 - c0), BF) for chosen, c0, c1 in wanted),
        [SMEM, ANY],
        (VMEM,) * len(wanted),
        [pltpu.SemaphoreType.DMA((len(flat),))],
        0,
        4 * rows * sum(c1 - c0 for *_, c0, c1 in flat),
        "pick",
    )(section_layers, in_hbm(train_weights))


def ring_copies(f, parts, c0, c1, dst, d0, sems, base):
    rows = parts[0].shape[0]
    n = 8
    copies = []
    for i, (distance, part) in enumerate(ORDER):
        size = parts[i].shape[0]
        at = pl.multiple_of(lax.rem(f + (distance + n), n) * rows + part * size, 16)
        copies.append(
            pltpu.make_async_copy(
                parts[i].at[:, pl.ds(c0, c1 - c0)],
                dst.at[pl.ds(at, size), pl.ds(d0, c1 - c0)],
                sems.at[base + i],
            )
        )
    return copies


def join(place, parts):
    count = len(parts)
    total, cols = 8 * parts[0].shape[0], parts[0].shape[1]

    def body(place_ref, *refs):
        ins, out, sems = refs[:count], refs[count], refs[count + 1]
        copies = ring_copies(place_ref[0], ins, 0, cols, out, 0, sems, 0)
        for c in copies:
            c.start()
        for c in copies:
            c.wait()

    return call(
        body,
        jax.ShapeDtypeStruct((total, cols), BF),
        [SMEM] + [ANY] * count,
        VMEM,
        [pltpu.SemaphoreType.DMA((count,))],
        0,
        4 * total * cols,
        "join",
    )(place, *[in_hbm(p) for p in parts])


def square_lanes(x):
    wide = x.astype(F32)
    squares = jnp.sum(wide * wide, axis=-1, keepdims=True)
    high = squares.astype(BF).astype(F32)
    lane = lax.broadcasted_iota(jnp.int32, (x.shape[0], 128), 1)
    return jnp.where(lane < 64, high, squares - high).astype(BF)


def first_project(x, place, parts):
    tokens, feats = x.shape
    half = tokens // 2
    count, cols = len(parts), parts[0].shape[1]

    def body(place_ref, x_ref, *refs):
        ins = refs[:count]
        mine_ref, other_ref, sq_ref, w, sems = refs[count:]
        copies = ring_copies(place_ref[0], ins, 0, cols, w, 0, sems, 0)
        for c in copies:
            c.start()
        mine_first = place_ref[1] == 0
        top, bottom = x_ref[:half], x_ref[half:]
        mine = jnp.where(mine_first, top, bottom)
        other = jnp.where(mine_first, bottom, top)
        sq_ref[...] = square_lanes(mine)
        for c in copies:
            c.wait()
        both = jnp.dot(jnp.concatenate([mine, other], axis=0), w[...], preferred_element_type=F32)
        mine_ref[...] = both[:half].astype(BF)
        other_ref[...] = both[half:].astype(BF)

    return call(
        body,
        (
            jax.ShapeDtypeStruct((half, cols), BF),
            jax.ShapeDtypeStruct((half, cols), BF),
            jax.ShapeDtypeStruct((half, 128), BF),
        ),
        [SMEM, VMEM] + [ANY] * count,
        (VMEM, VMEM, VMEM),
        [pltpu.VMEM((feats, cols), BF), pltpu.SemaphoreType.DMA((count,))],
        2 * tokens * feats * cols,
        2 * feats * cols,
        "first_project",
    )(place, x, *[in_hbm(p) for p in parts])


def bring(weights, slot, first, cols):
    blocks, cores, _, rows, _ = weights.shape

    def body(w_ref, out, sems):
        copies = [
            pltpu.make_async_copy(w_ref.at[:, i, slot, :, pl.ds(first, cols)], out.at[i], sems.at[i])
            for i in range(cores)
        ]
        for c in copies:
            c.start()
        for c in copies:
            c.wait()

    size = cores * blocks * rows * cols
    return call(
        body,
        pltpu.VMEM((cores, blocks, rows, cols), BF),
        [ANY],
        VMEM,
        [pltpu.SemaphoreType.DMA((cores,))],
        0,
        4 * size,
        "bring",
    )(in_hbm(weights))


def bring_turned(weights, slot, first, cols):
    blocks, cores, _, rows, _ = weights.shape

    def body(w_ref, out, w, sems):
        copies = [
            pltpu.make_async_copy(w_ref.at[:, i, slot, :, pl.ds(first, cols)], w.at[i], sems.at[i])
            for i in range(cores)
        ]
        for c in copies:
            c.start()
        for i in range(cores):
            copies[i].wait()
            out[i * cols : (i + 1) * cols, :] = w[i].reshape(blocks * rows, cols).T

    size = cores * blocks * rows * cols
    return call(
        body,
        pltpu.VMEM((cores * cols, blocks * rows), BF),
        [ANY],
        VMEM,
        [pltpu.VMEM((cores, blocks, rows, cols), BF), pltpu.SemaphoreType.DMA((cores,))],
        0,
        4 * size,
        "bring_turned",
    )(in_hbm(weights))


def project(x, terms, weights, slot=None, cols=None):
    tokens, feats = x.shape
    n = len(terms)
    inside = slot is not None
    if inside:
        blocks, cores, _, rows, _ = weights.shape
        weights = in_hbm(weights)
        terms = [in_hbm(r) for r in terms]
    else:
        cores, blocks, rows, cols = weights.shape

    def body(x_ref, *refs):
        term_refs = refs[:n]
        w, new_ref, pay_ref = refs[n : n + 3]
        copies = []
        if inside:
            source, (w, brought, sems) = w, refs[n + 3 :]
            copies = [
                pltpu.make_async_copy(source.at[:, i, slot, :, pl.ds(0, cols)], w.at[i], sems.at[i])
                for i in range(cores)
            ]
            first = [
                pltpu.make_async_copy(r, brought.at[i], sems.at[cores + i])
                for i, r in enumerate(term_refs)
            ]
            for c in first + copies:
                c.start()
            for c in first:
                c.wait()
            term_refs = [brought.at[i] for i in range(n)]
        total = x_ref[...].astype(F32)
        for r in term_refs:
            total = total + r[...].astype(F32)
        new = total.astype(BF)
        new_ref[...] = new
        pay_ref[:, cores * cols :] = square_lanes(new)
        for i in range(cores):
            for c in copies[i : i + 1]:
                c.wait()
            pay_ref[:, i * cols : (i + 1) * cols] = jnp.dot(
                new, w[i].reshape(feats, cols), preferred_element_type=F32
            ).astype(BF)

    return call(
        body,
        (
            jax.ShapeDtypeStruct((tokens, feats), BF),
            jax.ShapeDtypeStruct((tokens, cores * cols + 128), BF),
        ),
        [VMEM] + [ANY if inside else VMEM] * (n + 1),
        (VMEM, VMEM),
        [
            pltpu.VMEM((cores, blocks, rows, cols), BF),
            pltpu.VMEM((n, tokens, feats), BF),
            pltpu.SemaphoreType.DMA((cores + n,)),
        ]
        if inside
        else [],
        4 * tokens * feats * cols,
        4 * feats * cols,
        "project",
    )(x, *terms, weights)


def attend(payloads, place, lengths, cos_t, sin_t, weights, width, q_cols, kv_cols, last):
    n = len(payloads)
    seq = payloads[0].shape[0]
    n_in = len(weights)
    feats = weights[0].shape[0] if n_in == 2 else weights[0].shape[1]
    n_out = last or 1
    share = seq // n_out
    block = q_cols + 2 * kv_cols
    group = q_cols // HD

    def body(place_ref, len_ref, cos_ref, sin_ref, *refs):
        pays, w_refs, outs = refs[:n], refs[n : n + n_in], refs[n + n_in :]
        kv_refs = outs[n_out : n_out + 2]
        total = pays[0][...].astype(F32)
        for r in pays[1:]:
            total = total + r[...].astype(F32)
        squares = total[:, 2 * block : 2 * block + 1] + total[:, 2 * block + 64 : 2 * block + 65]
        factor = lax.rsqrt(squares / width + EPS)
        cos, sin = cos_ref[...] * factor, sin_ref[...] * factor

        def turned(vals):
            return (vals * cos + pltpu.roll(vals, HD // 2, 1) * sin).astype(BF)

        row = lax.broadcasted_iota(jnp.int32, (seq, seq), 0)
        col = lax.broadcasted_iota(jnp.int32, (seq, seq), 1)
        allowed = (col <= row) & (col < len_ref[place_ref[1]])
        allowed = jnp.concatenate([allowed] * group, axis=0)
        mixed = []
        for i, kv_ref in enumerate(kv_refs):
            at = i * block
            q = jnp.concatenate(
                [turned(total[:, at + h * HD : at + (h + 1) * HD]) for h in range(group)], axis=0
            )
            at += q_cols
            k = turned(total[:, at : at + kv_cols])
            v = (total[:, at + kv_cols : at + 2 * kv_cols] * factor).astype(BF)
            kv_ref[:, :kv_cols] = k
            kv_ref[:, kv_cols:] = v
            scores = lax.dot_general(
                q, k, (((1,), (1,)), ((), ())), preferred_element_type=F32
            ) * HD ** (-0.5)
            scores = jnp.where(allowed, scores, -1e30)
            top = jnp.max(scores, axis=-1, keepdims=True)
            raw = jnp.where(allowed, jnp.exp(scores - top), 0.0)
            probs = (raw / jnp.sum(raw, axis=-1, keepdims=True)).astype(BF)
            out = jnp.dot(probs, v, preferred_element_type=F32).astype(BF)
            mixed.append(
                jnp.concatenate([out[h * seq : (h + 1) * seq] for h in range(group)], axis=1)
            )
        if n_in == 1:
            part = jnp.dot(
                jnp.concatenate(mixed, axis=1), w_refs[0][...], preferred_element_type=F32
            )
        else:
            part = None
            for i in range(2):
                out = lax.dot_general(
                    mixed[i], w_refs[i][...], (((1,), (1,)), ((), ())), preferred_element_type=F32
                )
                part = out if part is None else part + out
        if not last:
            outs[0][...] = part.astype(BF)
            return
        whole = outs[-1]
        whole[...] = part
        for k in range(n_out):
            at = pl.multiple_of(lax.rem(place_ref[2] + k, n_out) * share, 8)
            outs[k][...] = whole[pl.ds(at, share), :].astype(BF)

    return call(
        body,
        (
            *[jax.ShapeDtypeStruct((share, feats), BF)] * n_out,
            jax.ShapeDtypeStruct((seq, 2 * kv_cols), BF),
            jax.ShapeDtypeStruct((seq, 2 * kv_cols), BF),
        ),
        [SMEM, SMEM, VMEM, VMEM] + [VMEM] * (n + n_in),
        (VMEM,) * (n_out + 2),
        [pltpu.VMEM((seq, feats), F32)] if last else [],
        4 * seq * feats * q_cols,
        4 * feats * q_cols,
        "attend",
    )(place, lengths, cos_t, sin_t, *payloads, *weights)


def residual(x, terms):
    total = x.astype(F32)
    for r in terms:
        total = total + r.astype(F32)
    return total.astype(BF)


def shards(train_weights, section_layers, prompt_embeds, prompt_lengths):
    n_fsdp = lax.axis_size("fsdp")
    n_section = lax.axis_size("section")
    n_tp = lax.axis_size("tp")
    f = lax.axis_index("fsdp")
    s = lax.axis_index("section")
    t = lax.axis_index("tp")
    core = t % 2
    rows = train_weights.shape[1]
    prompts, seq, width = prompt_embeds.shape
    q_cols = QH * HD // n_tp
    kv_cols = KVH * HD // n_tp
    block = q_cols + 2 * kv_cols
    feats = rows * n_fsdp

    place = jnp.stack([f, core, t // 2]).astype(jnp.int32)
    cols = block + q_cols
    calls = [(1, 2), (3,)]
    first_q, first_o, *later = pick(
        train_weights,
        section_layers,
        n_section,
        [((0,), 0, block), ((0,), block, cols)] + [(chosen, 0, cols) for chosen in calls],
    )
    flat = prompt_embeds.reshape(prompts * seq, width)
    x_all = jnp.concatenate(
        [
            lax.dynamic_slice_in_dim(flat, (k * n_section + s) * rows, rows, 1)
            for k in range(n_fsdp)
        ],
        axis=1,
    )
    x = lax.dynamic_slice_in_dim(x_all, core * seq, seq, 0)
    half_dim = HD // 2
    frequency = ROPE_BASE ** (-2.0 * jnp.arange(half_dim, dtype=F32) / HD)
    angles = jnp.arange(seq, dtype=F32)[:, None] * frequency[None, :]
    cosine, sine = jnp.cos(angles), jnp.sin(angles)
    cos_t = jnp.concatenate([cosine, cosine], axis=1)
    sin_t = jnp.concatenate([-sine, sine], axis=1)
    chips = [
        [k * n_tp + y * 2 + c for k in range(n_fsdp) for c in range(2)] for y in range(n_tp // 2)
    ]
    gathered = {}
    for chosen, piece in zip(calls, later):
        got = lax.all_gather(piece, ("fsdp", "tp"), axis=0, tiled=True, axis_index_groups=chips)
        for slot, layer in enumerate(chosen):
            gathered[layer] = (got.reshape(n_fsdp, 2, len(chosen), rows, cols), slot)

    q_ring, o_ring = Ring(first_q), Ring(first_o)
    q1 = q_ring.step()
    o1 = o_ring.step()
    q2 = q_ring.step(x_all)
    o2 = o_ring.step(cos_t, sin_t)
    q3 = q_ring.step(*o1)
    o_ring.step(*q2)
    q_ring.step(*o2)
    o_ring.step(*q3)

    states, caches = [], []
    terms = None
    for layer in range(n_section):
        last = layer + 1 == n_section
        if layer == 0:
            mine, other, squares = first_project(x_all, place, q_ring.got)
            payload = jnp.concatenate([mine, swap_core(other), squares], axis=1)
            o_own = join(place, [after(o_ring.got[0], payload)] + o_ring.got[1:])
            weights = (o_own, swap_core(o_own))
        else:
            array, slot = gathered[layer]
            if layer == 1:
                x, payload = project(x, terms, array, slot, block)
            else:
                x, payload = project(x, terms, bring(after(array, part[0]), slot, 0, block))
            states.append(x)
            weights = (bring_turned(after(array, payload), slot, block, q_cols),)
        payloads = [payload] + [shift(payload, "section", k) for k in (2, 1, 3)]
        *part, kv_first, kv_second = attend(
            payloads, place, prompt_lengths, cos_t, sin_t, weights,
            width, q_cols, kv_cols, n_tp // 2 if last else 0,
        )
        if layer == 0:
            caches.append((kv_first, kv_second))
        else:
            caches.append(
                (jnp.where(core == 0, kv_first, kv_second), jnp.where(core == 0, kv_second, kv_first))
            )
        terms = part[:1] + [shift(part[k if last else 0], "tp", 2 * k) for k in (2, 1, 3)]
    kv_own, kv_other = caches[0]
    for layer in range(1, n_section):
        kv_own = jnp.where(s == layer, caches[layer][0], kv_own)
        kv_other = jnp.where(s == layer, caches[layer][1], kv_other)
    kv_swapped = swap_core(kv_other)
    kv_out = jnp.where(
        core == 0, jnp.stack([kv_own, kv_swapped]), jnp.stack([kv_swapped, kv_own])
    ).reshape(1, prompts, seq, 2, kv_cols)
    terms[0] = after(terms[0], kv_out)
    chip_share = 2 * seq // n_tp
    final = residual(lax.dynamic_slice_in_dim(x, t // 2 * chip_share, chip_share, 0), terms)

    share = seq // n_tp
    keep, give = [], []
    for state in states:
        keep.append(lax.dynamic_slice_in_dim(state, t * share, share, 0))
        give.append(lax.dynamic_slice_in_dim(state, (t + 1 - 2 * core) * share, share, 0))
    keep.append(lax.dynamic_slice_in_dim(final, core * share, share, 0))
    give.append(lax.dynamic_slice_in_dim(final, (1 - core) * share, share, 0))
    keep, got = jnp.stack(keep), swap_core(jnp.stack(give))
    stacked = jnp.where(
        core == 0, jnp.concatenate([keep, got], axis=1), jnp.concatenate([got, keep], axis=1)
    )
    pieces = [None] * n_section
    for k in (2, 1, 3, 0):
        piece = lax.dynamic_index_in_dim(stacked, (s + k) % n_section, 0, keepdims=False)
        pieces[-k % n_section] = shift(piece, "section", k) if k else piece
    pieces = jnp.stack(pieces + pieces)
    pieces = lax.dynamic_slice_in_dim(pieces, (n_section - s) % n_section, n_section, 0)
    pieces = pieces.reshape(n_section, prompts * share, n_fsdp, rows)
    out = pieces.transpose(1, 2, 0, 3).reshape(1, prompts, share, width)
    return out, kv_out


def solution(mesh):
    in_specs = (P(None, ("fsdp", "section"), "tp"), P(), P("fsdp", None, None), P("fsdp"))
    out_specs = (P("section", "fsdp", "tp", None), P("section", "fsdp", None, None, "tp"))
    return jax.shard_map(shards, mesh=mesh, in_specs=in_specs, out_specs=out_specs, check_vma=False)
```

```python
import jax
import jax.numpy as jnp
from jax import lax
from jax.experimental import pallas as pl
from jax.experimental.pallas import tpu as pltpu
from jax.sharding import PartitionSpec as P

QH = 32
KVH = 8
HD = 128
ROPE_BASE = 1000000.0
EPS = 1e-06
BF = jnp.bfloat16
F32 = jnp.float32
VMEM_LIMIT = 16 * 1024 * 1024
ORDER = ((0, 0), (-1, 0), (1, 0), (-2, 0), (2, 0), (-3, 0), (3, 0), (4, 0), (4, 1))
ANY = pl.BlockSpec(memory_space=pl.ANY)
VMEM = pl.BlockSpec(memory_space=pltpu.VMEM)
SMEM = pl.BlockSpec(memory_space=pltpu.SMEM)


def shift(value, axis, by):
    n = lax.axis_size(axis)
    return lax.ppermute(value, axis, [(i, (i + by) % n) for i in range(n)])


def swap_core(value):
    n = lax.axis_size("tp")
    return lax.ppermute(value, "tp", [(i, i ^ 1) for i in range(n)])


def in_hbm(value):
    return pltpu.with_memory_space_constraint(value, pltpu.HBM)


def after(value, *others):
    return lax.optimization_barrier((value,) + others)[0]


class Ring:
    def __init__(self, block):
        self.half = block.shape[0] // 2
        self.got = [block]

    def step(self, *others):
        k = len(self.got) // 2
        up, down = (self.got[0], self.got[0]) if k == 0 else self.got[-2:]
        if k == 3:
            up, down = up[: self.half], down[self.half :]
        if others:
            up, down = after(up, *others), after(down, *others)
        pair = lax.optimization_barrier((shift(up, "fsdp", 1), shift(down, "fsdp", -1)))
        self.got += pair
        return pair


def call(body, out, in_specs, out_specs, scratch, flops, nbytes, name):
    return pl.pallas_call(
        body,
        out_shape=out,
        in_specs=in_specs,
        out_specs=out_specs,
        scratch_shapes=scratch,
        compiler_params=pltpu.CompilerParams(vmem_limit_bytes=VMEM_LIMIT),
        cost_estimate=pl.CostEstimate(flops=flops, bytes_accessed=nbytes, transcendentals=0),
        name=name,
    )


def pick(train_weights, section_layers, n_section, wanted):
    layers, rows, _ = train_weights.shape
    flat = [
        (out, at, layer, c0, c1)
        for out, (chosen, c0, c1) in enumerate(wanted)
        for at, layer in enumerate(chosen)
    ]

    def body(layers_ref, w_ref, *refs):
        outs, sems = refs[: len(wanted)], refs[len(wanted)]
        offsets = [jnp.int32(0)]
        for layer in range(n_section - 1):
            offsets.append(offsets[-1] + layers_ref[layer])
        copies = [
            pltpu.make_async_copy(
                w_ref.at[jnp.clip(offsets[layer], 0, layers - 1), :, pl.ds(c0, c1 - c0)],
                outs[out].at[pl.ds(at * rows, rows)],
                sems.at[i],
            )
            for i, (out, at, layer, c0, c1) in enumerate(flat)
        ]
        for c in copies:
            c.start()
        for c in copies:
            c.wait()

    return call(
        body,
        tuple(jax.ShapeDtypeStruct((len(chosen) * rows, c1 - c0), BF) for chosen, c0, c1 in wanted),
        [SMEM, ANY],
        (VMEM,) * len(wanted),
        [pltpu.SemaphoreType.DMA((len(flat),))],
        0,
        4 * rows * sum(c1 - c0 for *_, c0, c1 in flat),
        "pick",
    )(section_layers, in_hbm(train_weights))


def ring_copies(f, parts, c0, c1, dst, d0, sems, base):
    rows = parts[0].shape[0]
    n = 8
    copies = []
    for i, (distance, part) in enumerate(ORDER):
        size = parts[i].shape[0]
        at = pl.multiple_of(lax.rem(f + (distance + n), n) * rows + part * size, 16)
        copies.append(
            pltpu.make_async_copy(
                parts[i].at[:, pl.ds(c0, c1 - c0)],
                dst.at[pl.ds(at, size), pl.ds(d0, c1 - c0)],
                sems.at[base + i],
            )
        )
    return copies


def join(place, parts):
    count = len(parts)
    total, cols = 8 * parts[0].shape[0], parts[0].shape[1]

    def body(place_ref, *refs):
        ins, out, sems = refs[:count], refs[count], refs[count + 1]
        copies = ring_copies(place_ref[0], ins, 0, cols, out, 0, sems, 0)
        for c in copies:
            c.start()
        for c in copies:
            c.wait()

    return call(
        body,
        jax.ShapeDtypeStruct((total, cols), BF),
        [SMEM] + [ANY] * count,
        VMEM,
        [pltpu.SemaphoreType.DMA((count,))],
        0,
        4 * total * cols,
        "join",
    )(place, *[in_hbm(p) for p in parts])


def square_lanes(x):
    wide = x.astype(F32)
    squares = jnp.sum(wide * wide, axis=-1, keepdims=True)
    high = squares.astype(BF).astype(F32)
    lane = lax.broadcasted_iota(jnp.int32, (x.shape[0], 128), 1)
    return jnp.where(lane < 64, high, squares - high).astype(BF)


def first_project(x, place, parts):
    tokens, feats = x.shape
    half = tokens // 2
    count, cols = len(parts), parts[0].shape[1]

    def body(place_ref, x_ref, *refs):
        ins = refs[:count]
        mine_ref, other_ref, sq_ref, w, sems = refs[count:]
        copies = ring_copies(place_ref[0], ins, 0, cols, w, 0, sems, 0)
        for c in copies:
            c.start()
        mine_first = place_ref[1] == 0
        top, bottom = x_ref[:half], x_ref[half:]
        mine = jnp.where(mine_first, top, bottom)
        other = jnp.where(mine_first, bottom, top)
        sq_ref[...] = square_lanes(mine)
        for c in copies:
            c.wait()
        both = jnp.dot(jnp.concatenate([mine, other], axis=0), w[...], preferred_element_type=F32)
        mine_ref[...] = both[:half].astype(BF)
        other_ref[...] = both[half:].astype(BF)

    return call(
        body,
        (
            jax.ShapeDtypeStruct((half, cols), BF),
            jax.ShapeDtypeStruct((half, cols), BF),
            jax.ShapeDtypeStruct((half, 128), BF),
        ),
        [SMEM, VMEM] + [ANY] * count,
        (VMEM, VMEM, VMEM),
        [pltpu.VMEM((feats, cols), BF), pltpu.SemaphoreType.DMA((count,))],
        2 * tokens * feats * cols,
        2 * feats * cols,
        "first_project",
    )(place, x, *[in_hbm(p) for p in parts])


def bring(weights, slot, first, cols):
    blocks, cores, _, rows, _ = weights.shape

    def body(w_ref, out, sems):
        copies = [
            pltpu.make_async_copy(w_ref.at[:, i, slot, :, pl.ds(first, cols)], out.at[i], sems.at[i])
            for i in range(cores)
        ]
        for c in copies:
            c.start()
        for c in copies:
            c.wait()

    size = cores * blocks * rows * cols
    return call(
        body,
        pltpu.VMEM((cores, blocks, rows, cols), BF),
        [ANY],
        VMEM,
        [pltpu.SemaphoreType.DMA((cores,))],
        0,
        4 * size,
        "bring",
    )(in_hbm(weights))


def bring_turned(weights, slot, first, cols):
    blocks, cores, _, rows, _ = weights.shape

    def body(w_ref, out, w, sems):
        copies = [
            pltpu.make_async_copy(w_ref.at[:, i, slot, :, pl.ds(first, cols)], w.at[i], sems.at[i])
            for i in range(cores)
        ]
        for c in copies:
            c.start()
        for i in range(cores):
            copies[i].wait()
            out[i * cols : (i + 1) * cols, :] = w[i].reshape(blocks * rows, cols).T

    size = cores * blocks * rows * cols
    return call(
        body,
        pltpu.VMEM((cores * cols, blocks * rows), BF),
        [ANY],
        VMEM,
        [pltpu.VMEM((cores, blocks, rows, cols), BF), pltpu.SemaphoreType.DMA((cores,))],
        0,
        4 * size,
        "bring_turned",
    )(in_hbm(weights))


def project(x, terms, weights, slot=None, cols=None):
    tokens, feats = x.shape
    n = len(terms)
    inside = slot is not None
    if inside:
        blocks, cores, _, rows, _ = weights.shape
        weights = in_hbm(weights)
        terms = [in_hbm(r) for r in terms]
    else:
        cores, blocks, rows, cols = weights.shape

    def body(x_ref, *refs):
        term_refs = refs[:n]
        w, new_ref, pay_ref = refs[n : n + 3]
        copies = []
        if inside:
            source, (w, brought, sems) = w, refs[n + 3 :]
            copies = [
                pltpu.make_async_copy(source.at[:, i, slot, :, pl.ds(0, cols)], w.at[i], sems.at[i])
                for i in range(cores)
            ]
            first = [
                pltpu.make_async_copy(r, brought.at[i], sems.at[cores + i])
                for i, r in enumerate(term_refs)
            ]
            for c in first + copies:
                c.start()
            for c in first:
                c.wait()
            term_refs = [brought.at[i] for i in range(n)]
        total = x_ref[...].astype(F32)
        for r in term_refs:
            total = total + r[...].astype(F32)
        new = total.astype(BF)
        new_ref[...] = new
        pay_ref[:, cores * cols :] = square_lanes(new)
        for i in range(cores):
            for c in copies[i : i + 1]:
                c.wait()
            pay_ref[:, i * cols : (i + 1) * cols] = jnp.dot(
                new, w[i].reshape(feats, cols), preferred_element_type=F32
            ).astype(BF)

    return call(
        body,
        (
            jax.ShapeDtypeStruct((tokens, feats), BF),
            jax.ShapeDtypeStruct((tokens, cores * cols + 128), BF),
        ),
        [VMEM] + [ANY if inside else VMEM] * (n + 1),
        (VMEM, VMEM),
        [
            pltpu.VMEM((cores, blocks, rows, cols), BF),
            pltpu.VMEM((n, tokens, feats), BF),
            pltpu.SemaphoreType.DMA((cores + n,)),
        ]
        if inside
        else [],
        4 * tokens * feats * cols,
        4 * feats * cols,
        "project",
    )(x, *terms, weights)


def attend(payloads, place, lengths, cos_t, sin_t, weights, width, q_cols, kv_cols, last):
    n = len(payloads)
    seq = payloads[0].shape[0]
    n_in = len(weights)
    feats = weights[0].shape[0] if n_in == 2 else weights[0].shape[1]
    n_out = last or 1
    share = seq // n_out
    block = q_cols + 2 * kv_cols
    group = q_cols // HD

    def body(place_ref, len_ref, cos_ref, sin_ref, *refs):
        pays, w_refs, outs = refs[:n], refs[n : n + n_in], refs[n + n_in :]
        kv_refs = outs[n_out : n_out + 2]
        total = pays[0][...].astype(F32)
        for r in pays[1:]:
            total = total + r[...].astype(F32)
        squares = total[:, 2 * block : 2 * block + 1] + total[:, 2 * block + 64 : 2 * block + 65]
        factor = lax.rsqrt(squares / width + EPS)
        cos, sin = cos_ref[...] * factor, sin_ref[...] * factor

        def turned(vals):
            return (vals * cos + pltpu.roll(vals, HD // 2, 1) * sin).astype(BF)

        row = lax.broadcasted_iota(jnp.int32, (seq, seq), 0)
        col = lax.broadcasted_iota(jnp.int32, (seq, seq), 1)
        allowed = (col <= row) & (col < len_ref[place_ref[1]])
        allowed = jnp.concatenate([allowed] * group, axis=0)
        mixed = []
        for i, kv_ref in enumerate(kv_refs):
            at = i * block
            q = jnp.concatenate(
                [turned(total[:, at + h * HD : at + (h + 1) * HD]) for h in range(group)], axis=0
            )
            at += q_cols
            k = turned(total[:, at : at + kv_cols])
            v = (total[:, at + kv_cols : at + 2 * kv_cols] * factor).astype(BF)
            kv_ref[:, :kv_cols] = k
            kv_ref[:, kv_cols:] = v
            scores = lax.dot_general(
                q, k, (((1,), (1,)), ((), ())), preferred_element_type=F32
            ) * HD ** (-0.5)
            scores = jnp.where(allowed, scores, -1e30)
            top = jnp.max(scores, axis=-1, keepdims=True)
            raw = jnp.where(allowed, jnp.exp(scores - top), 0.0)
            probs = (raw / jnp.sum(raw, axis=-1, keepdims=True)).astype(BF)
            out = jnp.dot(probs, v, preferred_element_type=F32).astype(BF)
            mixed.append(
                jnp.concatenate([out[h * seq : (h + 1) * seq] for h in range(group)], axis=1)
            )
        if n_in == 1:
            part = jnp.dot(
                jnp.concatenate(mixed, axis=1), w_refs[0][...], preferred_element_type=F32
            )
        else:
            part = None
            for i in range(2):
                out = lax.dot_general(
                    mixed[i], w_refs[i][...], (((1,), (1,)), ((), ())), preferred_element_type=F32
                )
                part = out if part is None else part + out
        if not last:
            outs[0][...] = part.astype(BF)
            return
        whole = outs[-1]
        whole[...] = part
        for k in range(n_out):
            at = pl.multiple_of(lax.rem(place_ref[2] + k, n_out) * share, 8)
            outs[k][...] = whole[pl.ds(at, share), :].astype(BF)

    return call(
        body,
        (
            *[jax.ShapeDtypeStruct((share, feats), BF)] * n_out,
            jax.ShapeDtypeStruct((seq, 2 * kv_cols), BF),
            jax.ShapeDtypeStruct((seq, 2 * kv_cols), BF),
        ),
        [SMEM, SMEM, VMEM, VMEM] + [VMEM] * (n + n_in),
        (VMEM,) * (n_out + 2),
        [pltpu.VMEM((seq, feats), F32)] if last else [],
        4 * seq * feats * q_cols,
        4 * feats * q_cols,
        "attend",
    )(place, lengths, cos_t, sin_t, *payloads, *weights)


def residual(x, terms):
    total = x.astype(F32)
    for r in terms:
        total = total + r.astype(F32)
    return total.astype(BF)


def shards(train_weights, section_layers, prompt_embeds, prompt_lengths):
    n_fsdp = lax.axis_size("fsdp")
    n_section = lax.axis_size("section")
    n_tp = lax.axis_size("tp")
    f = lax.axis_index("fsdp")
    s = lax.axis_index("section")
    t = lax.axis_index("tp")
    core = t % 2
    rows = train_weights.shape[1]
    prompts, seq, width = prompt_embeds.shape
    q_cols = QH * HD // n_tp
    kv_cols = KVH * HD // n_tp
    block = q_cols + 2 * kv_cols
    feats = rows * n_fsdp

    place = jnp.stack([f, core, t // 2]).astype(jnp.int32)
    cols = block + q_cols
    calls = [(1, 2), (3,)]
    first_q, first_o, *later = pick(
        train_weights,
        section_layers,
        n_section,
        [((0,), 0, block), ((0,), block, cols)] + [(chosen, 0, cols) for chosen in calls],
    )
    flat = prompt_embeds.reshape(prompts * seq, width)
    x_all = jnp.concatenate(
        [
            lax.dynamic_slice_in_dim(flat, (k * n_section + s) * rows, rows, 1)
            for k in range(n_fsdp)
        ],
        axis=1,
    )
    x = lax.dynamic_slice_in_dim(x_all, core * seq, seq, 0)
    half_dim = HD // 2
    frequency = ROPE_BASE ** (-2.0 * jnp.arange(half_dim, dtype=F32) / HD)
    angles = jnp.arange(seq, dtype=F32)[:, None] * frequency[None, :]
    cosine, sine = jnp.cos(angles), jnp.sin(angles)
    cos_t = jnp.concatenate([cosine, cosine], axis=1)
    sin_t = jnp.concatenate([-sine, sine], axis=1)
    chips = [
        [k * n_tp + y * 2 + c for k in range(n_fsdp) for c in range(2)] for y in range(n_tp // 2)
    ]
    gathered = {}
    for chosen, piece in zip(calls, later):
        got = lax.all_gather(piece, ("fsdp", "tp"), axis=0, tiled=True, axis_index_groups=chips)
        for slot, layer in enumerate(chosen):
            gathered[layer] = (got.reshape(n_fsdp, 2, len(chosen), rows, cols), slot)

    q_ring, o_ring = Ring(first_q), Ring(first_o)
    q1 = q_ring.step()
    o1 = o_ring.step()
    q2 = q_ring.step(x_all)
    o2 = o_ring.step(cos_t, sin_t)
    q3 = q_ring.step(*o1)
    o_ring.step(*q2)
    q_ring.step(*o2)
    o_ring.step(*q3)

    states, caches = [], []
    terms = None
    for layer in range(n_section):
        last = layer + 1 == n_section
        if layer == 0:
            mine, other, squares = first_project(x_all, place, q_ring.got)
            payload = jnp.concatenate([mine, swap_core(other), squares], axis=1)
            o_own = join(place, [after(o_ring.got[0], payload)] + o_ring.got[1:])
            weights = (o_own, swap_core(o_own))
        else:
            array, slot = gathered[layer]
            if layer == 1:
                x, payload = project(x, terms, array, slot, block)
            else:
                x, payload = project(x, terms, bring(after(array, part[0]), slot, 0, block))
            states.append(x)
            weights = (bring_turned(after(array, payload), slot, block, q_cols),)
        payloads = [payload] + [shift(payload, "section", k) for k in (2, 1, 3)]
        *part, kv_first, kv_second = attend(
            payloads, place, prompt_lengths, cos_t, sin_t, weights,
            width, q_cols, kv_cols, n_tp // 2 if last else 0,
        )
        if layer == 0:
            caches.append((kv_first, kv_second))
        else:
            caches.append(
                (jnp.where(core == 0, kv_first, kv_second), jnp.where(core == 0, kv_second, kv_first))
            )
        terms = part[:1] + [shift(part[k if last else 0], "tp", 2 * k) for k in (2, 1, 3)]
    kv_own, kv_other = caches[0]
    for layer in range(1, n_section):
        kv_own = jnp.where(s == layer, caches[layer][0], kv_own)
        kv_other = jnp.where(s == layer, caches[layer][1], kv_other)
    kv_swapped = swap_core(kv_other)
    kv_out = jnp.where(
        core == 0, jnp.stack([kv_own, kv_swapped]), jnp.stack([kv_swapped, kv_own])
    ).reshape(1, prompts, seq, 2, kv_cols)
    terms[0] = after(terms[0], kv_out)
    chip_share = 2 * seq // n_tp
    final = residual(lax.dynamic_slice_in_dim(x, t // 2 * chip_share, chip_share, 0), terms)

    share = seq // n_tp
    keep, give = [], []
    for state in states:
        keep.append(lax.dynamic_slice_in_dim(state, t * share, share, 0))
        give.append(lax.dynamic_slice_in_dim(state, (t + 1 - 2 * core) * share, share, 0))
    keep.append(lax.dynamic_slice_in_dim(final, core * share, share, 0))
    give.append(lax.dynamic_slice_in_dim(final, (1 - core) * share, share, 0))
    keep, got = jnp.stack(keep), swap_core(jnp.stack(give))
    stacked = jnp.where(
        core == 0, jnp.concatenate([keep, got], axis=1), jnp.concatenate([got, keep], axis=1)
    )
    pieces = [None] * n_section
    for k in (2, 1, 3, 0):
        piece = lax.dynamic_index_in_dim(stacked, (s + k) % n_section, 0, keepdims=False)
        pieces[-k % n_section] = shift(piece, "section", k) if k else piece
    pieces = jnp.stack(pieces + pieces)
    pieces = lax.dynamic_slice_in_dim(pieces, (n_section - s) % n_section, n_section, 0)
    pieces = [pieces[k].reshape(prompts * share, n_fsdp, rows) for k in range(n_section)]
    out = jnp.concatenate(pieces, axis=-1).reshape(1, prompts, share, width)
    return out, kv_out


def solution(mesh):
    in_specs = (P(None, ("fsdp", "section"), "tp"), P(), P("fsdp", None, None), P("fsdp"))
    out_specs = (P("section", "fsdp", "tp", None), P("section", "fsdp", None, None, "tp"))
    return jax.shard_map(shards, mesh=mesh, in_specs=in_specs, out_specs=out_specs, check_vma=False)
```

```python
import jax
import jax.numpy as jnp
from jax import lax
from jax.experimental import pallas as pl
from jax.experimental.pallas import tpu as pltpu
from jax.sharding import PartitionSpec as P

QH = 32
KVH = 8
HD = 128
ROPE_BASE = 1000000.0
EPS = 1e-06
BF = jnp.bfloat16
F32 = jnp.float32
VMEM_LIMIT = 16 * 1024 * 1024
ORDER = ((0, 0), (-1, 0), (1, 0), (-2, 0), (2, 0), (-3, 0), (3, 0), (4, 0), (4, 1))
ANY = pl.BlockSpec(memory_space=pl.ANY)
VMEM = pl.BlockSpec(memory_space=pltpu.VMEM)
SMEM = pl.BlockSpec(memory_space=pltpu.SMEM)


def shift(value, axis, by):
    n = lax.axis_size(axis)
    return lax.ppermute(value, axis, [(i, (i + by) % n) for i in range(n)])


def swap_core(value):
    n = lax.axis_size("tp")
    return lax.ppermute(value, "tp", [(i, i ^ 1) for i in range(n)])


def in_hbm(value):
    return pltpu.with_memory_space_constraint(value, pltpu.HBM)


def after(value, *others):
    return lax.optimization_barrier((value,) + others)[0]


class Ring:
    def __init__(self, block):
        self.half = block.shape[0] // 2
        self.got = [block]

    def step(self, *others):
        k = len(self.got) // 2
        up, down = (self.got[0], self.got[0]) if k == 0 else self.got[-2:]
        if k == 3:
            up, down = up[: self.half], down[self.half :]
        if others:
            up, down = after(up, *others), after(down, *others)
        pair = lax.optimization_barrier((shift(up, "fsdp", 1), shift(down, "fsdp", -1)))
        self.got += pair
        return pair


def call(body, out, in_specs, out_specs, scratch, flops, nbytes, name):
    return pl.pallas_call(
        body,
        out_shape=out,
        in_specs=in_specs,
        out_specs=out_specs,
        scratch_shapes=scratch,
        compiler_params=pltpu.CompilerParams(vmem_limit_bytes=VMEM_LIMIT),
        cost_estimate=pl.CostEstimate(flops=flops, bytes_accessed=nbytes, transcendentals=0),
        name=name,
    )


def pick(train_weights, section_layers, n_section, wanted):
    layers, rows, _ = train_weights.shape
    flat = [
        (out, at, layer, c0, c1)
        for out, (chosen, c0, c1) in enumerate(wanted)
        for at, layer in enumerate(chosen)
    ]

    def body(layers_ref, w_ref, *refs):
        outs, sems = refs[: len(wanted)], refs[len(wanted)]
        offsets = [jnp.int32(0)]
        for layer in range(n_section - 1):
            offsets.append(offsets[-1] + layers_ref[layer])
        copies = [
            pltpu.make_async_copy(
                w_ref.at[jnp.clip(offsets[layer], 0, layers - 1), :, pl.ds(c0, c1 - c0)],
                outs[out].at[pl.ds(at * rows, rows)],
                sems.at[i],
            )
            for i, (out, at, layer, c0, c1) in enumerate(flat)
        ]
        for c in copies:
            c.start()
        for c in copies:
            c.wait()

    return call(
        body,
        tuple(jax.ShapeDtypeStruct((len(chosen) * rows, c1 - c0), BF) for chosen, c0, c1 in wanted),
        [SMEM, ANY],
        (VMEM,) * len(wanted),
        [pltpu.SemaphoreType.DMA((len(flat),))],
        0,
        4 * rows * sum(c1 - c0 for *_, c0, c1 in flat),
        "pick",
    )(section_layers, in_hbm(train_weights))


def ring_copies(f, parts, c0, c1, dst, d0, sems, base):
    rows = parts[0].shape[0]
    n = 8
    copies = []
    for i, (distance, part) in enumerate(ORDER):
        size = parts[i].shape[0]
        at = pl.multiple_of(lax.rem(f + (distance + n), n) * rows + part * size, 16)
        copies.append(
            pltpu.make_async_copy(
                parts[i].at[:, pl.ds(c0, c1 - c0)],
                dst.at[pl.ds(at, size), pl.ds(d0, c1 - c0)],
                sems.at[base + i],
            )
        )
    return copies


def join(place, parts):
    count = len(parts)
    total, cols = 8 * parts[0].shape[0], parts[0].shape[1]

    def body(place_ref, *refs):
        ins, out, sems = refs[:count], refs[count], refs[count + 1]
        copies = ring_copies(place_ref[0], ins, 0, cols, out, 0, sems, 0)
        for c in copies:
            c.start()
        for c in copies:
            c.wait()

    return call(
        body,
        jax.ShapeDtypeStruct((total, cols), BF),
        [SMEM] + [ANY] * count,
        VMEM,
        [pltpu.SemaphoreType.DMA((count,))],
        0,
        4 * total * cols,
        "join",
    )(place, *[in_hbm(p) for p in parts])


def square_lanes(x):
    wide = x.astype(F32)
    squares = jnp.sum(wide * wide, axis=-1, keepdims=True)
    high = squares.astype(BF).astype(F32)
    lane = lax.broadcasted_iota(jnp.int32, (x.shape[0], 128), 1)
    return jnp.where(lane < 64, high, squares - high).astype(BF)


def first_project(x, place, parts):
    tokens, feats = x.shape
    half = tokens // 2
    count, cols = len(parts), parts[0].shape[1]

    def body(place_ref, x_ref, *refs):
        ins = refs[:count]
        mine_ref, other_ref, sq_ref, w, sems = refs[count:]
        copies = ring_copies(place_ref[0], ins, 0, cols, w, 0, sems, 0)
        for c in copies:
            c.start()
        mine_first = place_ref[1] == 0
        top, bottom = x_ref[:half], x_ref[half:]
        mine = jnp.where(mine_first, top, bottom)
        other = jnp.where(mine_first, bottom, top)
        sq_ref[...] = square_lanes(mine)
        for c in copies:
            c.wait()
        both = jnp.dot(jnp.concatenate([mine, other], axis=0), w[...], preferred_element_type=F32)
        mine_ref[...] = both[:half].astype(BF)
        other_ref[...] = both[half:].astype(BF)

    return call(
        body,
        (
            jax.ShapeDtypeStruct((half, cols), BF),
            jax.ShapeDtypeStruct((half, cols), BF),
            jax.ShapeDtypeStruct((half, 128), BF),
        ),
        [SMEM, VMEM] + [ANY] * count,
        (VMEM, VMEM, VMEM),
        [pltpu.VMEM((feats, cols), BF), pltpu.SemaphoreType.DMA((count,))],
        2 * tokens * feats * cols,
        2 * feats * cols,
        "first_project",
    )(place, x, *[in_hbm(p) for p in parts])


def bring(weights, slot, first, cols):
    blocks, cores, _, rows, _ = weights.shape

    def body(w_ref, out, sems):
        copies = [
            pltpu.make_async_copy(w_ref.at[:, i, slot, :, pl.ds(first, cols)], out.at[i], sems.at[i])
            for i in range(cores)
        ]
        for c in copies:
            c.start()
        for c in copies:
            c.wait()

    size = cores * blocks * rows * cols
    return call(
        body,
        pltpu.VMEM((cores, blocks, rows, cols), BF),
        [ANY],
        VMEM,
        [pltpu.SemaphoreType.DMA((cores,))],
        0,
        4 * size,
        "bring",
    )(in_hbm(weights))


def bring_turned(weights, slot, first, cols):
    blocks, cores, _, rows, _ = weights.shape

    def body(w_ref, out, w, sems):
        copies = [
            pltpu.make_async_copy(w_ref.at[:, i, slot, :, pl.ds(first, cols)], w.at[i], sems.at[i])
            for i in range(cores)
        ]
        for c in copies:
            c.start()
        for i in range(cores):
            copies[i].wait()
            out[i * cols : (i + 1) * cols, :] = w[i].reshape(blocks * rows, cols).T

    size = cores * blocks * rows * cols
    return call(
        body,
        pltpu.VMEM((cores * cols, blocks * rows), BF),
        [ANY],
        VMEM,
        [pltpu.VMEM((cores, blocks, rows, cols), BF), pltpu.SemaphoreType.DMA((cores,))],
        0,
        4 * size,
        "bring_turned",
    )(in_hbm(weights))


def project(x, terms, weights, slot=None, cols=None):
    tokens, feats = x.shape
    n = len(terms)
    inside = slot is not None
    if inside:
        blocks, cores, _, rows, _ = weights.shape
        weights = in_hbm(weights)
        terms = [in_hbm(r) for r in terms]
    else:
        cores, blocks, rows, cols = weights.shape

    def body(x_ref, *refs):
        term_refs = refs[:n]
        w, new_ref, pay_ref = refs[n : n + 3]
        copies = []
        if inside:
            source, (w, brought, sems) = w, refs[n + 3 :]
            copies = [
                pltpu.make_async_copy(source.at[:, i, slot, :, pl.ds(0, cols)], w.at[i], sems.at[i])
                for i in range(cores)
            ]
            first = [
                pltpu.make_async_copy(r, brought.at[i], sems.at[cores + i])
                for i, r in enumerate(term_refs)
            ]
            for c in first + copies:
                c.start()
            for c in first:
                c.wait()
            term_refs = [brought.at[i] for i in range(n)]
        total = x_ref[...].astype(F32)
        for r in term_refs:
            total = total + r[...].astype(F32)
        new = total.astype(BF)
        new_ref[...] = new
        pay_ref[:, cores * cols :] = square_lanes(new)
        for i in range(cores):
            for c in copies[i : i + 1]:
                c.wait()
            pay_ref[:, i * cols : (i + 1) * cols] = jnp.dot(
                new, w[i].reshape(feats, cols), preferred_element_type=F32
            ).astype(BF)

    return call(
        body,
        (
            jax.ShapeDtypeStruct((tokens, feats), BF),
            jax.ShapeDtypeStruct((tokens, cores * cols + 128), BF),
        ),
        [VMEM] + [ANY if inside else VMEM] * (n + 1),
        (VMEM, VMEM),
        [
            pltpu.VMEM((cores, blocks, rows, cols), BF),
            pltpu.VMEM((n, tokens, feats), BF),
            pltpu.SemaphoreType.DMA((cores + n,)),
        ]
        if inside
        else [],
        4 * tokens * feats * cols,
        4 * feats * cols,
        "project",
    )(x, *terms, weights)


def attend(payloads, place, lengths, cos_t, sin_t, weights, width, q_cols, kv_cols, last):
    n = len(payloads)
    seq = payloads[0].shape[0]
    n_in = len(weights)
    feats = weights[0].shape[0] if n_in == 2 else weights[0].shape[1]
    n_out = last or 1
    share = seq // n_out
    block = q_cols + 2 * kv_cols
    group = q_cols // HD

    def body(place_ref, len_ref, cos_ref, sin_ref, *refs):
        pays, w_refs, outs = refs[:n], refs[n : n + n_in], refs[n + n_in :]
        kv_refs = outs[n_out : n_out + 2]
        total = pays[0][...].astype(F32)
        for r in pays[1:]:
            total = total + r[...].astype(F32)
        squares = total[:, 2 * block : 2 * block + 1] + total[:, 2 * block + 64 : 2 * block + 65]
        factor = lax.rsqrt(squares / width + EPS)
        cos, sin = cos_ref[...] * factor, sin_ref[...] * factor

        def turned(vals):
            return (vals * cos + pltpu.roll(vals, HD // 2, 1) * sin).astype(BF)

        row = lax.broadcasted_iota(jnp.int32, (seq, seq), 0)
        col = lax.broadcasted_iota(jnp.int32, (seq, seq), 1)
        allowed = (col <= row) & (col < len_ref[place_ref[1]])
        allowed = jnp.concatenate([allowed] * group, axis=0)
        mixed = []
        for i, kv_ref in enumerate(kv_refs):
            at = i * block
            q = jnp.concatenate(
                [turned(total[:, at + h * HD : at + (h + 1) * HD]) for h in range(group)], axis=0
            )
            at += q_cols
            k = turned(total[:, at : at + kv_cols])
            v = (total[:, at + kv_cols : at + 2 * kv_cols] * factor).astype(BF)
            kv_ref[:, :kv_cols] = k
            kv_ref[:, kv_cols:] = v
            scores = lax.dot_general(
                q, k, (((1,), (1,)), ((), ())), preferred_element_type=F32
            ) * HD ** (-0.5)
            scores = jnp.where(allowed, scores, -1e30)
            top = jnp.max(scores, axis=-1, keepdims=True)
            raw = jnp.where(allowed, jnp.exp(scores - top), 0.0)
            probs = (raw / jnp.sum(raw, axis=-1, keepdims=True)).astype(BF)
            out = jnp.dot(probs, v, preferred_element_type=F32).astype(BF)
            mixed.append(
                jnp.concatenate([out[h * seq : (h + 1) * seq] for h in range(group)], axis=1)
            )
        if n_in == 1:
            part = jnp.dot(
                jnp.concatenate(mixed, axis=1), w_refs[0][...], preferred_element_type=F32
            )
        else:
            part = None
            for i in range(2):
                out = lax.dot_general(
                    mixed[i], w_refs[i][...], (((1,), (1,)), ((), ())), preferred_element_type=F32
                )
                part = out if part is None else part + out
        if not last:
            outs[0][...] = part.astype(BF)
            return
        whole = outs[-1]
        whole[...] = part
        for k in range(n_out):
            at = pl.multiple_of(lax.rem(place_ref[2] + k, n_out) * share, 8)
            outs[k][...] = whole[pl.ds(at, share), :].astype(BF)

    return call(
        body,
        (
            *[jax.ShapeDtypeStruct((share, feats), BF)] * n_out,
            jax.ShapeDtypeStruct((seq, 2 * kv_cols), BF),
            jax.ShapeDtypeStruct((seq, 2 * kv_cols), BF),
        ),
        [SMEM, SMEM, VMEM, VMEM] + [VMEM] * (n + n_in),
        (VMEM,) * (n_out + 2),
        [pltpu.VMEM((seq, feats), F32)] if last else [],
        4 * seq * feats * q_cols,
        4 * feats * q_cols,
        "attend",
    )(place, lengths, cos_t, sin_t, *payloads, *weights)


def residual(x, terms):
    total = x.astype(F32)
    for r in terms:
        total = total + r.astype(F32)
    return total.astype(BF)


def shards(train_weights, section_layers, prompt_embeds, prompt_lengths):
    n_fsdp = lax.axis_size("fsdp")
    n_section = lax.axis_size("section")
    n_tp = lax.axis_size("tp")
    f = lax.axis_index("fsdp")
    s = lax.axis_index("section")
    t = lax.axis_index("tp")
    core = t % 2
    rows = train_weights.shape[1]
    prompts, seq, width = prompt_embeds.shape
    q_cols = QH * HD // n_tp
    kv_cols = KVH * HD // n_tp
    block = q_cols + 2 * kv_cols
    feats = rows * n_fsdp

    place = jnp.stack([f, core, t // 2]).astype(jnp.int32)
    cols = block + q_cols
    calls = [(1, 2), (3,)]
    first_q, first_o, *later = pick(
        train_weights,
        section_layers,
        n_section,
        [((0,), 0, block), ((0,), block, cols)] + [(chosen, 0, cols) for chosen in calls],
    )
    flat = prompt_embeds.reshape(prompts * seq, width)
    x_all = jnp.concatenate(
        [
            lax.dynamic_slice_in_dim(flat, (k * n_section + s) * rows, rows, 1)
            for k in range(n_fsdp)
        ],
        axis=1,
    )
    x = lax.dynamic_slice_in_dim(x_all, core * seq, seq, 0)
    half_dim = HD // 2
    frequency = ROPE_BASE ** (-2.0 * jnp.arange(half_dim, dtype=F32) / HD)
    angles = jnp.arange(seq, dtype=F32)[:, None] * frequency[None, :]
    cosine, sine = jnp.cos(angles), jnp.sin(angles)
    cos_t = jnp.concatenate([cosine, cosine], axis=1)
    sin_t = jnp.concatenate([-sine, sine], axis=1)
    chips = [
        [k * n_tp + y * 2 + c for k in range(n_fsdp) for c in range(2)] for y in range(n_tp // 2)
    ]
    gathered = {}
    for chosen, piece in zip(calls, later):
        got = lax.all_gather(piece, ("fsdp", "tp"), axis=0, tiled=True, axis_index_groups=chips)
        for slot, layer in enumerate(chosen):
            gathered[layer] = (got.reshape(n_fsdp, 2, len(chosen), rows, cols), slot)

    q_ring, o_ring = Ring(first_q), Ring(first_o)
    q1 = q_ring.step()
    o1 = o_ring.step()
    q2 = q_ring.step(x_all)
    o2 = o_ring.step(cos_t, sin_t)
    q3 = q_ring.step(*o1)
    o_ring.step(*q2)
    q_ring.step(*o2)
    o_ring.step(*q3)

    states, caches = [], []
    terms = None
    for layer in range(n_section):
        last = layer + 1 == n_section
        if layer == 0:
            mine, other, squares = first_project(x_all, place, q_ring.got)
            payload = jnp.concatenate([mine, swap_core(other), squares], axis=1)
            o_own = join(place, [after(o_ring.got[0], payload)] + o_ring.got[1:])
            weights = (o_own, swap_core(o_own))
        else:
            array, slot = gathered[layer]
            if layer == 1:
                x, payload = project(x, terms, array, slot, block)
            else:
                x, payload = project(x, terms, bring(after(array, part[0]), slot, 0, block))
            states.append(x)
            weights = (bring_turned(after(array, payload), slot, block, q_cols),)
        payloads = [payload] + [shift(payload, "section", k) for k in (2, 1, 3)]
        *part, kv_first, kv_second = attend(
            payloads, place, prompt_lengths, cos_t, sin_t, weights,
            width, q_cols, kv_cols, n_tp // 2 if last else 0,
        )
        if layer == 0:
            caches.append((kv_first, kv_second))
        else:
            caches.append(
                (jnp.where(core == 0, kv_first, kv_second), jnp.where(core == 0, kv_second, kv_first))
            )
        terms = part[:1] + [shift(part[k if last else 0], "tp", 2 * k) for k in (2, 1, 3)]
    kv_own, kv_other = caches[0]
    for layer in range(1, n_section):
        kv_own = jnp.where(s == layer, caches[layer][0], kv_own)
        kv_other = jnp.where(s == layer, caches[layer][1], kv_other)
    kv_swapped = swap_core(kv_other)
    kv_out = jnp.where(
        core == 0, jnp.stack([kv_own, kv_swapped]), jnp.stack([kv_swapped, kv_own])
    ).reshape(1, prompts, seq, 2, kv_cols)
    terms[0] = after(terms[0], kv_out)
    chip_share = 2 * seq // n_tp
    final = residual(lax.dynamic_slice_in_dim(x, t // 2 * chip_share, chip_share, 0), terms)

    share = seq // n_tp
    keep, give = [], []
    for state in states:
        keep.append(lax.dynamic_slice_in_dim(state, t * share, share, 0))
        give.append(lax.dynamic_slice_in_dim(state, (t + 1 - 2 * core) * share, share, 0))
    keep.append(lax.dynamic_slice_in_dim(final, core * share, share, 0))
    give.append(lax.dynamic_slice_in_dim(final, (1 - core) * share, share, 0))
    keep, got = jnp.stack(keep), swap_core(jnp.stack(give))
    stacked = jnp.where(
        core == 0, jnp.concatenate([keep, got], axis=1), jnp.concatenate([got, keep], axis=1)
    )
    order = (2, 1, 3, 0)
    sent = lax.optimization_barrier(
        tuple(
            lax.dynamic_index_in_dim(stacked, (s + k) % n_section, 0, keepdims=False) for k in order
        )
    )
    pieces = [None] * n_section
    for k, piece in zip(order, sent):
        pieces[-k % n_section] = shift(piece, "section", k) if k else piece
    pieces = jnp.stack(pieces + pieces)
    pieces = lax.dynamic_slice_in_dim(pieces, (n_section - s) % n_section, n_section, 0)
    pieces = [pieces[k].reshape(prompts * share, n_fsdp, rows) for k in range(n_section)]
    out = jnp.concatenate(pieces, axis=-1).reshape(1, prompts, share, width)
    return out, kv_out


def solution(mesh):
    in_specs = (P(None, ("fsdp", "section"), "tp"), P(), P("fsdp", None, None), P("fsdp"))
    out_specs = (P("section", "fsdp", "tp", None), P("section", "fsdp", None, None, "tp"))
    return jax.shard_map(shards, mesh=mesh, in_specs=in_specs, out_specs=out_specs, check_vma=False)
```
